256 devices in a mesh: row: 8 (over x, core), feat: 32 (over y, z).
Axes of the slice: x: 4, y: 4, z: 8, core: 2. Of those that a mesh axis runs over, the one named last changes fastest.
Arguments:
- doc_scores: float32 [262144], P(('row', 'feat')), may hold values from -8 to 8
- doc_labels: int32 [262144], P(('row', 'feat')), may hold values from 0 to 4
- doc_ranks: int32 [262144], P(('row', 'feat')), may hold values from 0 to 1023, as said below
- query_tiles: int32 [8, 64], P('row'), may hold values from 1 to 8, as said below
- bin_codes: int32 [2048, 262144], P('feat', 'row'), may hold values from 0 to 255
Outputs:
- gradient: float32 [262144], P(('row', 'feat'))
- hessian: float32 [262144], P(('row', 'feat'))
- histogram: float32 [2048, 2, 256], P('feat')
- split_gain: float32 [2048], P('feat')
The draws below stay inside these ranges and needn't reach their ends.
Inputs may be any that keep to these rules, and one draw needn't show every extreme that they name: `query_tiles`: in every slab the counts sum to 256; every slab has at least one query of 1 tile and one of 8 tiles. `doc_ranks`: within a query of c tiles the ranks of its documents are 0 to 128 c - 1, each once.
All inputs are finite; a program needn't handle non-finite values.
Results may differ from the reference program's by a relative error of at most 0.0045.
Values may be sent and summed in bfloat16 or wider, within the bound.
A program may use at most 64 MiB of HBM per device.

```python
import jax
import jax.numpy as jnp
from jax import lax

F = 2048
BINS = 256
MAX_TILES = 8
SLAB_ROWS = 32768
QUERIES = 64
SLABS = 8
ROWS = 262144


def one_slab_tiles(slab_key):
    spare = MAX_TILES - 1
    extras = SLAB_ROWS // 128 - QUERIES - spare
    order_key, slot_key = jax.random.split(slab_key)
    order = jax.random.permutation(order_key, QUERIES)
    largest = order[0]
    smallest = order[1]
    slot_query = jnp.arange(QUERIES * spare, dtype=jnp.int32) // spare
    blocked = (slot_query == largest) | (slot_query == smallest)
    priority = jax.random.permutation(slot_key, QUERIES * spare).astype(jnp.int32)
    priority = jnp.where(blocked, priority + QUERIES * spare, priority)
    chosen = jnp.argsort(priority)[:extras]
    filled = jnp.zeros((QUERIES * spare,), jnp.int32).at[chosen].set(1)
    per_query = jnp.sum(filled.reshape(QUERIES, spare), axis=1)
    return 1 + per_query + spare * (jnp.arange(QUERIES, dtype=jnp.int32) == largest).astype(jnp.int32)


def all_tiles(base_key):
    slab_keys = jax.random.split(jax.random.fold_in(base_key, 11), SLABS)
    return jax.vmap(one_slab_tiles)(slab_keys)


def one_slab_ranks(tile_counts, slab_key):
    sizes = tile_counts * 128
    starts = jnp.cumsum(sizes) - sizes
    positions = jnp.arange(SLAB_ROWS, dtype=jnp.int32)
    query_ids = jnp.sum((positions[None, :] >= starts[:, None]).astype(jnp.int32), axis=0) - 1
    shuffle = jax.random.permutation(slab_key, SLAB_ROWS).astype(jnp.int32)
    order = jnp.argsort(query_ids * SLAB_ROWS + shuffle)
    placed = jnp.zeros((SLAB_ROWS,), jnp.int32).at[order].set(positions)
    return placed - starts[query_ids]


def draw_query_tiles(key, part):
    return all_tiles(key)


def draw_doc_ranks(key, part):
    tiles = all_tiles(key)
    slab_keys = jax.random.split(jax.random.fold_in(key, 23), SLABS)
    return jax.vmap(one_slab_ranks)(tiles, slab_keys).reshape(-1)


def touch_ends(drawn, key, low, high):
    longest = drawn.shape.index(max(drawn.shape))
    spots = []
    for shift in (0, 1):
        where = [jax.random.randint(jax.random.fold_in(key, axis), (), 0, length) for axis, length in enumerate(drawn.shape)]
        where[longest] = (where[longest] + shift) % drawn.shape[longest]
        spots.append(tuple(where))
    return drawn.at[spots[0]].set(low).at[spots[1]].set(high)


def block_levels(stream_key, shape, cuts, low, top_value):
    gain, own = 1.0, jax.random.fold_in(stream_key, 6)
    for dim, parts in cuts:
        draws = jnp.exp(jax.random.uniform(jax.random.fold_in(own, dim), (parts,), jnp.float32, low / len(cuts), top_value / len(cuts)))
        gain = gain * jnp.repeat(draws, shape[dim] // parts).reshape([-1 if axis == dim else 1 for axis in range(len(shape))])
    return gain


def gaussian(own_key, extent, width, most, pieces=(), held_as=jnp.bfloat16):
    level = block_levels(own_key, extent, pieces, -0.22, 0.18) if pieces else 1.0
    values = jax.random.normal(own_key, extent, jnp.float32) * width * level
    return jnp.minimum(jnp.maximum(values, -most), most).astype(held_as)


def setup_inputs(seed: int = 0) -> dict:
    seeds = jax.random.split(jax.random.key(seed), 6)
    doc_scores = gaussian(seeds[0], (ROWS,), 2.0, 8.0, ((0, 256),), jnp.float32)
    doc_labels = touch_ends(jax.random.randint(seeds[1], (ROWS,), 0, 5), jax.random.fold_in(seeds[1], 1), 0, 4).astype(jnp.int32)
    doc_ranks = draw_doc_ranks(jax.random.fold_in(seeds[5], 71), 0)
    query_tiles = draw_query_tiles(jax.random.fold_in(seeds[5], 71), 0)
    bin_codes = touch_ends(jax.random.randint(seeds[4], (F, ROWS), 0, BINS), jax.random.fold_in(seeds[4], 1), 0, BINS - 1).astype(jnp.int32)
    return dict(doc_scores=doc_scores, doc_labels=doc_labels, doc_ranks=doc_ranks, query_tiles=query_tiles, bin_codes=bin_codes)


LEVEL_GAINS = (0.0, 1.0, 3.0, 7.0, 15.0)


def gain_of(labels_in):
    totals = jnp.zeros(labels_in.shape, jnp.float32)
    for level in range(5):
        totals = totals + jnp.where(labels_in == level, jnp.float32(LEVEL_GAINS[level]), jnp.float32(0.0))
    return totals


def disc_of(ranks_in):
    return 1.0 / jnp.log2(ranks_in.astype(jnp.float32) + 2.0)


def prefix_table(longest):
    places = jnp.arange(longest, dtype=jnp.int32).astype(jnp.float32)
    values = 1.0 / jnp.log2(places + 2.0)
    return jnp.concatenate([jnp.zeros((1,), jnp.float32), jnp.cumsum(values)])


def lookup(table, where_float):
    places = jnp.arange(table.shape[0], dtype=jnp.int32).astype(jnp.float32)
    equal = places == where_float[..., None]
    return jnp.sum(jnp.where(equal, table, jnp.float32(0.0)), axis=-1)


def query_norms(gains, sizes, starts, longest):
    count_docs = gains.shape[0]
    positions = jnp.arange(count_docs, dtype=jnp.int32)
    query_ids = jnp.sum((positions[None, :] >= starts[:, None]).astype(jnp.int32), axis=0) - 1
    member = (query_ids[None, :] == jnp.arange(sizes.shape[0], dtype=jnp.int32)[:, None]).astype(jnp.float32)
    levels = jnp.array(LEVEL_GAINS, jnp.float32)
    level_hot = (gains[:, None] == levels[None, :]).astype(jnp.float32)
    counts = jnp.dot(member, level_hot, precision=lax.Precision.HIGHEST)
    upper = (jnp.arange(5, dtype=jnp.int32)[None, :] > jnp.arange(5, dtype=jnp.int32)[:, None]).astype(jnp.float32)
    higher = jnp.sum(counts[:, None, :] * upper[None, :, :], axis=2)
    table = prefix_table(longest)
    ideal = jnp.sum(levels[None, :] * (lookup(table, higher + counts) - lookup(table, higher)), axis=1)
    return 1.0 + ideal


def pair_sums(score_row, gain_row, disc_row, score_col, gain_col, disc_col, valid_col, norm_value):
    diff = score_row[:, None] - score_col[None, :]
    weight = jnp.abs(gain_row[:, None] - gain_col[None, :]) * jnp.abs(disc_row[:, None] - disc_col[None, :]) / norm_value
    weight = weight * valid_col[None, :]
    rising = jax.nn.sigmoid(diff)
    falling = jax.nn.sigmoid(-diff)
    zeroes = jnp.zeros_like(weight)
    terms = jnp.where(gain_row[:, None] > gain_col[None, :], -weight * falling,
                      jnp.where(gain_row[:, None] < gain_col[None, :], weight * rising, zeroes))
    return jnp.sum(terms, axis=1), jnp.sum(weight * rising * falling, axis=1)


def slab_lambdas(packed):
    scores_slab, gains_slab, discs_slab, tiles_slab = packed
    count_docs = scores_slab.shape[0]
    longest = MAX_TILES * 128
    sizes = (tiles_slab * 128).astype(jnp.int32)
    starts = (jnp.cumsum(sizes) - sizes).astype(jnp.int32)
    norms = query_norms(gains_slab, sizes, starts, longest)
    filler = jnp.zeros((longest,), jnp.float32)
    padded_scores = jnp.concatenate([scores_slab, filler])
    padded_gains = jnp.concatenate([gains_slab, filler])
    padded_discs = jnp.concatenate([discs_slab, filler])
    window_ids = jnp.arange(longest, dtype=jnp.int32)

    def one_query(carried, query):
        begin = starts[query]
        window_scores = lax.dynamic_slice_in_dim(padded_scores, begin, longest)
        window_gains = lax.dynamic_slice_in_dim(padded_gains, begin, longest)
        window_discs = lax.dynamic_slice_in_dim(padded_discs, begin, longest)
        valid = (window_ids < sizes[query]).astype(jnp.float32)
        grads, hessians = pair_sums(window_scores, window_gains, window_discs,
                                    window_scores, window_gains, window_discs, valid, norms[query])
        update = jnp.stack([grads * valid, hessians * valid])
        current = lax.dynamic_slice(carried, (jnp.int32(0), begin), (2, longest))
        return lax.dynamic_update_slice(carried, current + update, (jnp.int32(0), begin)), None

    initial = jnp.zeros((2, count_docs + longest), jnp.float32)
    result, unused = lax.scan(one_query, initial, jnp.arange(sizes.shape[0], dtype=jnp.int32))
    return result[:, :count_docs]


def best_gains(hist):
    running = jnp.cumsum(hist, axis=2)
    grad_left = running[:, 0, :-1]
    hess_left = running[:, 1, :-1]
    grad_all = running[:, 0, -1:]
    hess_all = running[:, 1, -1:]
    grad_right = grad_all - grad_left
    gains = grad_left * grad_left / (hess_left + 1.0) + grad_right * grad_right / (hess_all - hess_left + 1.0) - grad_all * grad_all / (hess_all + 1.0)
    return jnp.max(gains, axis=1)


def reference(doc_scores, doc_labels, doc_ranks, query_tiles, bin_codes):
    slab_count = query_tiles.shape[0]
    per_slab = doc_scores.shape[0] // slab_count
    gains = gain_of(doc_labels)
    discs = disc_of(doc_ranks)
    lambdas_all = lax.map(slab_lambdas, (doc_scores.reshape(slab_count, per_slab), gains.reshape(slab_count, per_slab),
                                         discs.reshape(slab_count, per_slab), query_tiles))
    gradient = lambdas_all[:, 0, :].reshape(-1)
    hessian = lambdas_all[:, 1, :].reshape(-1)
    rounded = lax.optimization_barrier(jnp.stack([gradient, hessian], axis=1).astype(jnp.bfloat16)).astype(jnp.float32)

    def feature_hist(code_row):
        return jax.ops.segment_sum(rounded, code_row, num_segments=BINS).T

    histogram = lax.map(feature_hist, bin_codes)
    best = best_gains(histogram)
    split_gain = best / (jnp.max(best) + 1e-6)
    return gradient, hessian, histogram, split_gain
```

```python
import functools

import jax
import jax.experimental.pallas as pl
import jax.experimental.pallas.tpu as pltpu
import jax.numpy as jnp
from jax import lax
from jax.sharding import PartitionSpec as P

BINS = 256
MAX_TILES = 8
LANES = 128
QUERIES = 64
HIGH, LOW = 8, 32
GROUP = 8
MESH = pl.DeviceIdType.MESH
F32, BF16, F8, I8 = jnp.float32, jnp.bfloat16, jnp.float8_e4m3fn, jnp.int8


def iota(shape, dim):
    return lax.broadcasted_iota(jnp.int32, shape, dim)


def pieces(x):
    first = x.astype(BF16)
    rest = x - first.astype(F32)
    second = rest.astype(BF16)
    third = (rest - second.astype(F32)).astype(BF16)
    return first, second, third


def lambda_kernel(feats, tiles_ref, score_ref, label_ref, rank_ref, grad_ref, hess_ref, all_ref,
                  window, wide, sums, gathered, halo_send, halo_recv, send, recv):
    me = lax.axis_index("feat")
    left, right = lax.rem(me + feats - 1, feats), lax.rem(me + 1, feats)
    barrier = pltpu.get_barrier_semaphore()

    @pl.loop(1, feats)
    def _(step):
        pl.semaphore_signal(barrier, inc=1, device_id={"feat": lax.rem(me + step, feats)}, device_id_type=MESH)

    odds = jnp.exp(score_ref[...])
    gains = (jnp.left_shift(1, label_ref[...]) - 1).astype(F32)
    discs = 1.0 / jnp.log2(rank_ref[...].astype(F32) + 2.0)
    own = (odds, gains, discs)
    for which in range(3):
        window[which, 8:16, :] = own[which]
    pl.semaphore_wait(barrier, feats - 1)
    halos = []
    for side, (target, place) in enumerate(((left, 16), (right, 0))):
        copy = pltpu.make_async_remote_copy(
            src_ref=window.at[:, pl.ds(8, 8), :], dst_ref=window.at[:, pl.ds(place, 8), :],
            send_sem=halo_send.at[side], recv_sem=halo_recv.at[side],
            device_id={"feat": target}, device_id_type=MESH)
        copy.start()
        halos.append(copy)

    first = [jnp.int32(0)] * 8
    count = [jnp.int32(1)] * 8
    start = 8 - me * 8
    for query in range(QUERIES):
        tiles = tiles_ref[0, query]
        for tile in range(8):
            inside = start <= 8 + tile
            first[tile] = jnp.where(inside, start, first[tile])
            count[tile] = jnp.where(inside, tiles, count[tile])
        start = start + tiles

    for which in range(3):
        turned = jnp.transpose(own[which])
        for tile in range(8):
            wide[which, tile] = jnp.broadcast_to(turned[:, tile:tile + 1], (LANES, LANES))

    place = (iota((8, LANES), 0) * LANES + iota((8, LANES), 1)).astype(F32)
    table = 1.0 / jnp.log2(place + 2.0)
    rows = iota((8, LANES), 0)
    first_rows, count_rows = jnp.zeros((8, LANES), jnp.int32), jnp.zeros((8, LANES), jnp.int32)
    for tile in range(8):
        first_rows = jnp.where(rows == tile, first[tile], first_rows)
        count_rows = jnp.where(rows == tile, count[tile], count_rows)

    for copy in halos:
        copy.wait()

    ones = jnp.ones((LANES, LANES), BF16)
    all_gains = window[1]
    reach = jnp.concatenate([(all_gains >= F32(2 ** level - 1)).astype(F32) for level in range(1, 5)], axis=0)
    reach = jnp.dot(reach.astype(BF16), ones, preferred_element_type=F32)
    above = [jnp.zeros((8, LANES), F32)] * 4
    for tile in range(24):
        member = (first_rows <= tile) & (first_rows + count_rows > tile)
        for level in range(4):
            at = level * 24 + tile
            above[level] = above[level] + jnp.where(member, jnp.broadcast_to(reach[at:at + 1], (8, LANES)), 0.0)
    ideals = []
    for tile in range(8):
        total = jnp.zeros((8, LANES), F32)
        for level in range(4):
            limit = jnp.broadcast_to(above[level][tile:tile + 1], (8, LANES))
            total = total + jnp.where(place < limit, table * F32(2 ** level), 0.0)
        ideals.append(jnp.sum(total, axis=0, keepdims=True))
    ideal = jnp.sum(jnp.concatenate(ideals, axis=0), axis=1, keepdims=True)
    scale = 1.0 / (1.0 + ideal)

    lanes = iota((LANES, LANES), 1)
    totals = jnp.zeros((LANES, LANES), F32)
    for tile in range(8):
        columns = []
        for step in range(MAX_TILES):
            at = jnp.minimum(jnp.maximum(first[tile] + step, 0), 23)
            columns.append([window[which, pl.ds(at, 1), :] for which in range(3)]
                           + [jnp.where(step < count[tile], F32(1), F32(0))])

        @pl.loop(0, LANES // 16)
        def _(part):
            here = pl.ds(pl.multiple_of(part * 16, 16), 16)
            odds_i, gain_i, disc_i = (wide[which, tile, here, :] for which in range(3))
            grad = jnp.zeros((16, LANES), F32)
            hess = jnp.zeros((16, LANES), F32)
            for odds_j, gain_j, disc_j, valid in columns:
                inverse = pl.reciprocal(odds_i + odds_j, approx=True)
                delta = gain_i - gain_j
                weight = delta * (jnp.abs(disc_i - disc_j) * (inverse * valid))
                grad = grad + weight * jnp.where(delta > 0, odds_j, odds_i)
                hess = hess + jnp.abs(weight) * (inverse * odds_j)
            sums[0, here, :] = grad
            sums[1, here, :] = hess

        for which in range(2):
            high = sums[which].astype(BF16)
            low = (sums[which] - high.astype(F32)).astype(BF16)
            added = (jnp.dot(high, ones, preferred_element_type=F32)
                     + jnp.dot(low, ones, preferred_element_type=F32))
            totals = jnp.where(lanes == which * 8 + tile, added, totals)
    totals = jnp.transpose(totals)
    gradient = -totals[0:8] * scale
    hessian = totals[8:16] * (odds * scale)
    grad_ref[...] = gradient
    hess_ref[...] = hessian
    gathered[me] = jnp.concatenate([gradient, hessian], axis=0).astype(BF16)

    def exchange(step):
        target = lax.rem(me + step, feats)
        return pltpu.make_async_remote_copy(
            src_ref=gathered.at[me], dst_ref=gathered.at[me], send_sem=send.at[step], recv_sem=recv.at[step],
            device_id={"feat": target}, device_id_type=MESH)

    @pl.loop(1, feats)
    def _(step):
        exchange(step).start()

    @pl.loop(1, feats)
    def _(step):
        exchange(step).wait()

    all_ref[...] = gathered[...]


def lambdas(feats, tiles, scores, labels, ranks):
    block = jax.ShapeDtypeStruct((8, LANES), F32)
    vmem = pl.BlockSpec(memory_space=pltpu.VMEM)
    return pl.pallas_call(
        functools.partial(lambda_kernel, feats),
        out_shape=(block, block, jax.ShapeDtypeStruct((feats, 16, LANES), BF16)),
        in_specs=[pl.BlockSpec(memory_space=pltpu.SMEM), vmem, vmem, vmem],
        out_specs=(vmem, vmem, vmem),
        scratch_shapes=[
            pltpu.VMEM((3, 24, LANES), F32), pltpu.VMEM((3, 8, LANES, LANES), F32), pltpu.VMEM((2, LANES, LANES), F32),
            pltpu.VMEM((feats, 16, LANES), BF16),
            pltpu.SemaphoreType.DMA((2,)), pltpu.SemaphoreType.DMA((2,)),
            pltpu.SemaphoreType.DMA((feats,)), pltpu.SemaphoreType.DMA((feats,)),
        ],
        compiler_params=pltpu.CompilerParams(collective_id=0, has_side_effects=True, vmem_limit_bytes=32 * 2 ** 20),
        name="lambdas",
    )(tiles, scores, labels, ranks)


def histogram_kernel(groups, docs, unroll, lam_ref, codes_ref, out_ref, codes, spread, sems):
    def fetch(group):
        slot = lax.rem(group, 3)
        return pltpu.make_async_copy(
            codes_ref.at[pl.ds(pl.multiple_of(group * GROUP, GROUP), GROUP), :], codes.at[slot], sems.at[slot])

    for group in range(3):
        fetch(group).start()

    @pl.loop(0, docs // 1024)
    def _(owner):
        part = lam_ref[owner].astype(F32)
        for which in range(2):
            for tile in range(8):
                at = pl.ds(pl.multiple_of(owner * 1024 + tile * LANES, LANES), LANES)
                row = which * 8 + tile
                spread[which, :, at] = jnp.broadcast_to(part[row:row + 1], (16, LANES)).astype(BF16)

    def body(*accs):
        zero = jnp.zeros((), BF16)

        @pl.loop(0, groups)
        def _(group):
            fetch(group).wait()
            slot = lax.rem(group, 3)

            def one(chunk, acc, mxu):
                at = pl.ds(pl.multiple_of(chunk * BINS, BINS), BINS)
                code = codes[slot, :, at]
                high = (code >> 5).astype(F32)
                high = jnp.concatenate([high, high - 1.0], axis=0).astype(BF16)
                hits = [high == jnp.array(2 * k, BF16) for k in range(HIGH // 2)]
                lhs = jnp.concatenate(
                    [jnp.where(hit, spread[which, :, at], zero) for which in range(2) for hit in hits], axis=0)
                low = code & (LOW - 1)
                low = jnp.concatenate([low - k for k in range(4)], axis=0).astype(I8)
                rhs = jnp.concatenate(
                    [jnp.where(low == jnp.array(4 * k, I8), jnp.ones((), F8), jnp.zeros((), F8)) for k in range(LOW // 4)],
                    axis=0)
                pltpu.matmul_push_rhs(rhs, 0, mxu, transpose=True)
                pltpu.matmul_acc_lhs(acc, lhs, load_staged_rhs=0)

            half = docs // BINS // 2

            @pl.loop(0, half // unroll)
            def _(turn):
                for k in range(unroll):
                    for mxu in range(2):
                        one(mxu * half + turn * unroll + k, accs[mxu], mxu)

            @pl.when(group + 3 < groups)
            def _():
                fetch(group + 3).start()

            total = (pltpu.matmul_pop(accs[0]) + pltpu.matmul_pop(accs[1])).reshape(2 * HIGH, GROUP, BINS)
            shape = (2 * HIGH, GROUP, BINS)
            same = iota(shape, 1) == (iota(shape, 2) & (GROUP - 1))
            out_ref[group] = jnp.sum(jnp.where(same, total, 0.0), axis=1)

    pl.run_scoped(body, *[pltpu.ACC(mxu)((2 * HIGH * GROUP, BINS), F32) for mxu in range(2)])


def histograms(lam, codes, unroll=4):
    feats_here, docs = codes.shape
    groups = feats_here // GROUP
    return pl.pallas_call(
        functools.partial(histogram_kernel, groups, docs, unroll),
        out_shape=jax.ShapeDtypeStruct((groups, 2 * HIGH, BINS), F32),
        in_specs=[pl.BlockSpec(memory_space=pltpu.VMEM), pl.BlockSpec(memory_space=pltpu.HBM)],
        out_specs=pl.BlockSpec(memory_space=pltpu.VMEM),
        scratch_shapes=[
            pltpu.VMEM((3, GROUP, docs), jnp.int32), pltpu.VMEM((2, 16, docs), BF16), pltpu.SemaphoreType.DMA((3,))],
        compiler_params=pltpu.CompilerParams(vmem_limit_bytes=32 * 2 ** 20),
        name="histograms",
    )(lam, codes)


def gain_kernel(rows, feats, part_ref, hist_ref, gain_ref,
                parts, blocks, bests, tops, peaks, send_a, recv_a, send_b, recv_b, send_c, recv_c, send_d, recv_d,
                send_e, recv_e):
    row, feat = lax.axis_index("row"), lax.axis_index("feat")
    barrier = pltpu.get_barrier_semaphore()

    @pl.loop(1, rows)
    def _(step):
        pl.semaphore_signal(barrier, inc=1, device_id={"row": lax.rem(row + step, rows)}, device_id_type=MESH)

    @pl.loop(1, feats)
    def _(step):
        pl.semaphore_signal(barrier, inc=1, device_id={"feat": lax.rem(feat + step, feats)}, device_id_type=MESH)

    source, target = iota((BINS, BINS), 0), iota((BINS, BINS), 1)
    source_low, source_feat = source // GROUP, source % GROUP
    target_feat, target_low = target // LOW, target % LOW
    same = source_feat == target_feat
    as_bf16 = lambda flag: jnp.where(flag, F32(1), F32(0)).astype(BF16)
    move = as_bf16(same & (source_low == target_low))
    prefix = as_bf16(same & (source_low <= target_low))
    whole = as_bf16(same)
    parts[row] = part_ref[row]
    pl.semaphore_wait(barrier, rows + feats - 2)

    def scatter(step):
        to = lax.rem(row + step, rows)
        return pltpu.make_async_remote_copy(
            src_ref=part_ref.at[to], dst_ref=parts.at[row], send_sem=send_a.at[step], recv_sem=recv_a.at[step],
            device_id={"row": to}, device_id_type=MESH)

    @pl.loop(1, rows)
    def _(step):
        scatter(step).start()

    @pl.loop(1, rows)
    def _(step):
        scatter(step).wait()

    summed = parts[0]
    for k in range(1, rows):
        summed = summed + parts[k]

    split = jnp.concatenate(pieces(summed), axis=0)

    def product(matrix):
        full = jnp.dot(split, matrix, preferred_element_type=F32)
        return full[0:16] + (full[16:32] + full[32:48])

    moved, left, across = product(move), product(prefix), product(whole)
    running = [jnp.zeros((1, BINS), F32)] * 2
    sides = [[], []]
    for which in range(2):
        for k in range(HIGH):
            at = which * HIGH + k
            sides[which].append(left[at:at + 1] + running[which])
            running[which] = running[which] + across[at:at + 1]
    grad_left, hess_left = (jnp.concatenate(side, axis=0) for side in sides)
    grad_all, hess_all = running
    grad_right = grad_all - grad_left
    gain = (grad_left * grad_left / (hess_left + 1.0)
            + grad_right * grad_right / (hess_all - hess_left + 1.0)
            - grad_all * grad_all / (hess_all + 1.0))
    shape = (HIGH, BINS)
    last = (iota(shape, 0) == HIGH - 1) & (iota(shape, 1) % LOW == LOW - 1)
    gain = jnp.where(last, -jnp.inf, gain)
    best = jnp.max(gain, axis=0, keepdims=True)
    for shift in (1, 2, 4, 8, 16):
        best = jnp.maximum(best, pltpu.roll(best, BINS - shift, 1))
    heads = iota((1, BINS), 1) % LOW == 0
    best = jnp.where(heads, best, -jnp.inf)
    top = jnp.max(best, axis=1, keepdims=True)
    tops[feat] = jnp.broadcast_to(top, (1, LANES))
    bests[row] = jnp.where(heads, best, 0.0)

    def spread_top(step):
        return pltpu.make_async_remote_copy(
            src_ref=tops.at[feat], dst_ref=tops.at[feat], send_sem=send_b.at[step], recv_sem=recv_b.at[step],
            device_id={"feat": lax.rem(feat + step, feats)}, device_id_type=MESH)

    @pl.loop(1, feats)
    def _(step):
        spread_top(step).start()

    block = iota(shape, 1) // LOW == iota(shape, 0)
    for which in range(2):
        whole_rows = moved[which * HIGH:(which + 1) * HIGH]
        placed = jnp.zeros(shape, F32)
        for shift in range(GROUP):
            turned = whole_rows if shift == 0 else pltpu.roll(whole_rows, shift * LOW, 1)
            turned = jnp.where(block, turned, 0.0)
            placed = placed + (turned if shift == 0 else pltpu.roll(turned, GROUP - shift, 0))
        blocks[row, :, which, :] = placed

    def to_rows(step, ref, send_sem, recv_sem):
        return pltpu.make_async_remote_copy(
            src_ref=ref.at[row], dst_ref=ref.at[row], send_sem=send_sem.at[step], recv_sem=recv_sem.at[step],
            device_id={"row": lax.rem(row + step, rows)}, device_id_type=MESH)

    @pl.loop(1, rows)
    def _(step):
        to_rows(step, blocks, send_c, recv_c).start()
        to_rows(step, bests, send_d, recv_d).start()

    @pl.loop(1, feats)
    def _(step):
        spread_top(step).wait()

    peaks[row] = jnp.max(tops[...], axis=0)

    @pl.loop(1, rows)
    def _(step):
        to_rows(step, peaks, send_e, recv_e).start()

    @pl.loop(1, rows)
    def _(step):
        to_rows(step, blocks, send_c, recv_c).wait()
        to_rows(step, bests, send_d, recv_d).wait()
    for k in range(rows):
        hist_ref[k * GROUP:(k + 1) * GROUP] = blocks[k]

    @pl.loop(1, rows)
    def _(step):
        to_rows(step, peaks, send_e, recv_e).wait()
    largest = jnp.max(jnp.max(peaks[...], axis=0), axis=1, keepdims=True)
    pick = as_bf16((source[:, :LANES] % LOW == 0) & (source[:, :LANES] // LOW == iota((BINS, LANES), 1) % GROUP))
    every = jnp.concatenate([bests[k] for k in range(rows)], axis=0)
    chosen = [jnp.dot(piece, pick, preferred_element_type=F32) for piece in pieces(every)]
    chosen = chosen[0] + (chosen[1] + chosen[2])
    mine = iota((rows, LANES), 1) // GROUP == iota((rows, LANES), 0)
    line = jnp.sum(jnp.where(mine, chosen, 0.0), axis=0, keepdims=True)
    gain_ref[...] = (line / (largest + 1e-6))[:, :rows * GROUP]


def gains_of(rows, feats, part):
    vmem = pl.BlockSpec(memory_space=pltpu.VMEM)
    groups = part.shape[0]
    dma = pltpu.SemaphoreType.DMA
    return pl.pallas_call(
        functools.partial(gain_kernel, rows, feats),
        out_shape=(jax.ShapeDtypeStruct((groups * GROUP, 2, BINS), F32), jax.ShapeDtypeStruct((1, groups * GROUP), F32)),
        in_specs=[vmem],
        out_specs=(vmem, vmem),
        scratch_shapes=[
            pltpu.VMEM((rows, 2 * HIGH, BINS), F32), pltpu.VMEM((rows, GROUP, 2, BINS), F32),
            pltpu.VMEM((rows, 1, BINS), F32), pltpu.VMEM((feats, 1, LANES), F32), pltpu.VMEM((rows, 1, LANES), F32),
            dma((rows,)), dma((rows,)), dma((feats,)), dma((feats,)), dma((rows,)), dma((rows,)),
            dma((rows,)), dma((rows,)), dma((rows,)), dma((rows,)),
        ],
        compiler_params=pltpu.CompilerParams(collective_id=1, has_side_effects=True, vmem_limit_bytes=32 * 2 ** 20),
        name="gains",
    )(part)


def shards(rows, feats, doc_scores, doc_labels, doc_ranks, query_tiles, bin_codes):
    tile_of = lambda x: x.reshape(8, LANES)
    gradient, hessian, lam = lambdas(feats, query_tiles, tile_of(doc_scores), tile_of(doc_labels), tile_of(doc_ranks))
    part = histograms(lam, bin_codes)
    histogram, split_gain = gains_of(rows, feats, part)
    return gradient.reshape(-1), hessian.reshape(-1), histogram, split_gain.reshape(-1)


def solution(mesh):
    return jax.shard_map(
        functools.partial(shards, mesh.shape["row"], mesh.shape["feat"]),
        mesh=mesh,
        in_specs=(P(("row", "feat")), P(("row", "feat")), P(("row", "feat")), P("row", None), P("feat", "row")),
        out_specs=(P(("row", "feat")), P(("row", "feat")), P("feat", None, None), P("feat")),
        check_vma=False,
    )
```

```python
import functools

import jax
import jax.experimental.pallas as pl
import jax.experimental.pallas.tpu as pltpu
import jax.numpy as jnp
from jax import lax
from jax.sharding import PartitionSpec as P

BINS = 256
MAX_TILES = 8
LANES = 128
QUERIES = 64
HIGH, LOW = 8, 32
GROUP = 8
MESH = pl.DeviceIdType.MESH
F32, BF16, F8, I8 = jnp.float32, jnp.bfloat16, jnp.float8_e4m3fn, jnp.int8


def iota(shape, dim):
    return lax.broadcasted_iota(jnp.int32, shape, dim)


def pieces(x):
    first = x.astype(BF16)
    rest = x - first.astype(F32)
    second = rest.astype(BF16)
    third = (rest - second.astype(F32)).astype(BF16)
    return first, second, third


def query_spans(tiles_ref, me):
    first = [jnp.int32(0)] * 8
    count = [jnp.int32(1)] * 8
    start = 8 - me * 8
    for query in range(QUERIES):
        tiles = tiles_ref[0, query]
        for tile in range(8):
            inside = start <= 8 + tile
            first[tile] = jnp.where(inside, start, first[tile])
            count[tile] = jnp.where(inside, tiles, count[tile])
        start = start + tiles
    return first, count


def discount_table():
    place = (iota((8, LANES), 0) * LANES + iota((8, LANES), 1)).astype(F32)
    return place, 1.0 / jnp.log2(place + 2.0)


def query_scale(window, first, count):
    place, table = discount_table()
    rows = iota((8, LANES), 0)
    first_rows, count_rows = jnp.zeros((8, LANES), jnp.int32), jnp.zeros((8, LANES), jnp.int32)
    for tile in range(8):
        first_rows = jnp.where(rows == tile, first[tile], first_rows)
        count_rows = jnp.where(rows == tile, count[tile], count_rows)
    all_gains = window[1]
    reach = jnp.concatenate([(all_gains >= F32(2 ** level - 1)).astype(F32) for level in range(1, 5)], axis=0)
    reach = jnp.broadcast_to(jnp.sum(reach, axis=1, keepdims=True), (96, LANES))
    above = [jnp.zeros((8, LANES), F32)] * 4
    for tile in range(24):
        member = (first_rows <= tile) & (first_rows + count_rows > tile)
        for level in range(4):
            at = level * 24 + tile
            above[level] = above[level] + jnp.where(member, jnp.broadcast_to(reach[at:at + 1], (8, LANES)), 0.0)
    ideals = []
    for tile in range(8):
        total = jnp.zeros((8, LANES), F32)
        for level in range(4):
            limit = jnp.broadcast_to(above[level][tile:tile + 1], (8, LANES))
            total = total + jnp.where(place < limit, table * F32(2 ** level), 0.0)
        ideals.append(jnp.sum(total, axis=0, keepdims=True))
    ideal = jnp.sum(jnp.concatenate(ideals, axis=0), axis=1, keepdims=True)
    return 1.0 / (1.0 + ideal)


def widen(window, wide, slot):
    for which in range(3):
        turned = jnp.transpose(window[which, slot * 8:slot * 8 + 8, :])
        for tile in range(8):
            wide[which, slot * 8 + tile] = jnp.broadcast_to(turned[:, tile:tile + 1], (LANES, LANES))


def pair_sums(own, wide, first, count):
    odds, gains, discs = own
    grads, hessians = [], []
    rows = 32
    for tile in range(8):
        odds_i, gain_i, disc_i = (jnp.broadcast_to(x[tile:tile + 1], (rows, LANES)) for x in own)

        def column(step, carried):
            at = jnp.minimum(jnp.maximum(first[tile] + step, 0), 23)
            valid = jnp.where(step < count[tile], F32(1), F32(0))
            grad, hess = carried
            for part in range(0, LANES, rows):
                odds_j, gain_j, disc_j = (wide[which, at, part:part + rows, :] for which in range(3))
                inverse = pl.reciprocal(odds_i + odds_j, approx=True)
                delta = gain_i - gain_j
                weight = delta * (jnp.abs(disc_i - disc_j) * (inverse * valid))
                grad = grad + weight * jnp.where(delta > 0, odds_j, odds_i)
                hess = hess + jnp.abs(weight) * (inverse * odds_j)
            return grad, hess

        empty = jnp.zeros((rows, LANES), F32)
        grad, hess = lax.fori_loop(0, MAX_TILES, column, (empty, empty))
        grads.append(jnp.sum(grad, axis=0, keepdims=True))
        hessians.append(jnp.sum(hess, axis=0, keepdims=True))
    return jnp.concatenate(grads, axis=0), jnp.concatenate(hessians, axis=0)


def build_matrices(matrices):
    source, target = iota((BINS, BINS), 0), iota((BINS, BINS), 1)
    source_low, source_feat = source >> 3, source & 7
    target_feat, target_low = target >> 5, target & 31
    same = source_feat == target_feat
    for k, flag in enumerate((same & (source_low == target_low), same & (source_low <= target_low), same)):
        matrices[k] = jnp.where(flag, F32(1), F32(0)).astype(BF16)
    pick = ((source & (LOW - 1)) == 0) & ((source >> 5) == (target & 7))
    matrices[3] = jnp.where(pick, F32(1), F32(0)).astype(BF16)


def round_kernel(rows, ys, zs, *refs):
    accumulators = ([pltpu.ACC(k % 2)((2 * HIGH * GROUP, BINS), F32) for k in range(rows)]
                    + [pltpu.ACC(k % 2)((48, BINS), F32) for k in range(3)] + [pltpu.ACC(0)((32, BINS), F32)])
    pl.run_scoped(lambda *accs: round_body(rows, ys, zs, accs[:rows], accs[rows:], *refs), *accumulators)


def round_body(rows, ys, zs, accs, small, tiles_hbm, score_hbm, label_hbm, rank_hbm, codes_hbm,
                 grad_ref, hess_ref, hist_ref, gain_ref,
                 tiles_ref, score_ref, label_ref, rank_ref, codes,
                 window, wide, gathered, spread, matrices, mine, parts, blocks, bests, tops_z, tops_y,
                 in_sem, code_sem, halo_send, halo_recv, send_z, recv_z, send_y, recv_y,
                 send_a, recv_a, send_b, recv_b, send_c, recv_c, send_d, recv_d, send_e, recv_e):
    row, feat = lax.axis_index("row"), lax.axis_index("feat")
    feats = ys * zs
    y, z = feat // zs, lax.rem(feat, zs)
    groups = codes.shape[0] // GROUP
    chunks = codes.shape[1] // 1024

    loads = [pltpu.make_async_copy(src, dst, in_sem.at[k]) for k, (src, dst) in enumerate(
        ((score_hbm, score_ref), (label_hbm, label_ref), (rank_hbm, rank_ref), (tiles_hbm, tiles_ref)))]
    for load in loads:
        load.start()
    code_loads = [pltpu.make_async_copy(codes_hbm.at[pl.ds(k * GROUP, GROUP), :], codes.at[pl.ds(k * GROUP, GROUP), :],
                                        code_sem.at[k]) for k in range(groups)]

    barrier = pltpu.get_barrier_semaphore()

    def at_row(step):
        return {"row": lax.rem(row + step, rows)}

    def at_z(step):
        return {"feat": y * zs + lax.rem(z + step, zs)}

    def at_y(step):
        return {"feat": lax.rem(y + step, ys) * zs + z}

    def at_feat(step):
        return {"feat": lax.rem(feat + step, feats)}

    def signal(device):
        pl.semaphore_signal(barrier, inc=1, device_id=device, device_id_type=MESH)

    signal(at_feat(1))
    signal(at_feat(feats - 1))
    for step in range(1, zs):
        signal(at_z(step))
    for step in range(1, ys):
        signal(at_y(step))
    for step in range(1, rows):
        signal(at_row(step))
    for load in loads:
        load.wait()
    for load in code_loads:
        load.start()

    odds = jnp.exp(score_ref[...])
    gains = (jnp.left_shift(1, label_ref[...]) - 1).astype(F32)
    discs = 1.0 / jnp.log2(rank_ref[...].astype(F32) + 2.0)
    own = (odds, gains, discs)
    for which in range(3):
        window[which, 8:16, :] = own[which]
    build_matrices(matrices)
    pl.semaphore_wait(barrier, 2 + zs - 1 + ys - 1 + rows - 1)
    halos = []
    for side, (target, place) in enumerate(((feats - 1, 16), (1, 0))):
        copy = pltpu.make_async_remote_copy(
            src_ref=window.at[:, pl.ds(8, 8), :], dst_ref=window.at[:, pl.ds(place, 8), :],
            send_sem=halo_send.at[side], recv_sem=halo_recv.at[side],
            device_id=at_feat(target), device_id_type=MESH)
        copy.start()
        halos.append(copy)
    first, count = query_spans(tiles_ref, feat)
    widen(window, wide, 1)
    for copy in halos:
        copy.wait()
    widen(window, wide, 0)
    widen(window, wide, 2)
    scale = query_scale(window, first, count)
    grad, hess = pair_sums(own, wide, first, count)
    grad = -grad * scale
    hess = hess * (odds * scale)
    grad_ref[...] = grad
    hess_ref[...] = hess
    gathered[feat] = jnp.concatenate([grad, hess], axis=0).astype(BF16)

    def over_z(step):
        return pltpu.make_async_remote_copy(
            src_ref=gathered.at[feat], dst_ref=gathered.at[feat], send_sem=send_z.at[step], recv_sem=recv_z.at[step],
            device_id=at_z(step), device_id_type=MESH)

    def over_y(step):
        block = gathered.at[pl.ds(y * zs, zs)]
        return pltpu.make_async_remote_copy(
            src_ref=block, dst_ref=block, send_sem=send_y.at[step], recv_sem=recv_y.at[step],
            device_id=at_y(step), device_id_type=MESH)

    for step in range(1, zs):
        over_z(step).start()
    for load in code_loads:
        load.wait()

    def scatter(group):
        return pltpu.make_async_remote_copy(
            src_ref=mine.at[group], dst_ref=parts.at[row], send_sem=send_a.at[group], recv_sem=recv_a.at[row],
            device_id={"row": jnp.int32(group)}, device_id_type=MESH)

    def arrival(step):
        source = lax.rem(row + step, rows)
        return pltpu.make_async_remote_copy(
            src_ref=parts.at[source], dst_ref=parts.at[source], send_sem=send_a.at[source], recv_sem=recv_a.at[source],
            device_id=at_row(step), device_id_type=MESH)

    zero = jnp.zeros((), BF16)

    @pl.loop(0, chunks)
    def _(turn):
        @pl.when(turn == 1)
        def _():
            for step in range(1, zs):
                over_z(step).wait()
            for step in range(1, ys):
                over_y(step).start()

        for step in range(1, ys):
            @pl.when(turn == step * zs)
            def _():
                over_y(ys - step).wait()

        owner = lax.rem(y + turn // zs, ys) * zs + lax.rem(z + lax.rem(turn, zs), zs)
        part = gathered[owner].astype(F32)
        for which in range(2):
            for tile in range(8):
                line = which * 8 + tile
                spread[which, :, tile * LANES:(tile + 1) * LANES] = jnp.broadcast_to(
                    part[line:line + 1], (16, LANES)).astype(BF16)
        for k in range(1024 // BINS):
            at = pl.ds(pl.multiple_of(owner * 1024 + k * BINS, BINS), BINS)
            lam = [spread[which, :, k * BINS:(k + 1) * BINS] for which in range(2)]
            for group in range(groups):
                code = codes[group * GROUP:(group + 1) * GROUP, at]
                high = (code >> 5).astype(F32)
                high = jnp.concatenate([high, high - 1.0], axis=0).astype(BF16)
                hits = [high == jnp.array(2 * k, BF16) for k in range(HIGH // 2)]
                lhs = jnp.concatenate([jnp.where(hit, value, zero) for value in lam for hit in hits], axis=0)
                low = code & (LOW - 1)
                low = jnp.concatenate([low - k for k in range(4)], axis=0).astype(I8)
                rhs = jnp.concatenate(
                    [jnp.where(low == jnp.array(4 * k, I8), jnp.ones((), F8), jnp.zeros((), F8))
                     for k in range(LOW // 4)], axis=0)
                stage = group // 2 % 2
                pltpu.matmul_push_rhs(rhs, stage, group % 2, transpose=True)
                pltpu.matmul_acc_lhs(accs[group], lhs, load_staged_rhs=stage)

    shape = (2 * HIGH, GROUP, BINS)
    same = iota(shape, 1) == (iota(shape, 2) & (GROUP - 1))
    for group in range(groups):
        total = pltpu.matmul_pop(accs[group]).reshape(shape)
        mine[group] = jnp.sum(jnp.where(same, total, 0.0), axis=1)

        @pl.when(row != group)
        def _():
            scatter(group).start()


    parts[row] = mine[row]
    for step in range(1, rows):
        arrival(step).wait_recv()
    summed = parts[0]
    for k in range(1, rows):
        summed = summed + parts[k]

    split = jnp.concatenate(pieces(summed), axis=0)
    for k in range(3):
        pltpu.matmul_push_rhs(matrices[k], k // 2, k % 2)
        pltpu.matmul_acc_lhs(small[k], split, load_staged_rhs=k // 2)

    def product(k):
        full = pltpu.matmul_pop(small[k])
        return full[0:16] + (full[16:32] + full[32:48])

    left, across, moved = product(1), product(2), product(0)
    running = [jnp.zeros((1, BINS), F32)] * 2
    sides = [[], []]
    for which in range(2):
        for k in range(HIGH):
            at = which * HIGH + k
            sides[which].append(left[at:at + 1] + running[which])
            running[which] = running[which] + across[at:at + 1]
    grad_left, hess_left = (jnp.concatenate(side, axis=0) for side in sides)
    grad_all, hess_all = running
    grad_right = grad_all - grad_left
    gain = (grad_left * grad_left / (hess_left + 1.0)
            + grad_right * grad_right / (hess_all - hess_left + 1.0)
            - grad_all * grad_all / (hess_all + 1.0))
    shape = (HIGH, BINS)
    last = (iota(shape, 0) == HIGH - 1) & ((iota(shape, 1) & (LOW - 1)) == LOW - 1)
    gain = jnp.where(last, -jnp.inf, gain)
    best = jnp.max(gain, axis=0, keepdims=True)
    for shift in (1, 2, 4, 8, 16):
        best = jnp.maximum(best, pltpu.roll(best, BINS - shift, 1))
    heads = (iota((1, BINS), 1) & (LOW - 1)) == 0
    bests[row] = jnp.where(heads, best, 0.0)

    def to_rows(step, ref, send_sem, recv_sem):
        return pltpu.make_async_remote_copy(
            src_ref=ref.at[row], dst_ref=ref.at[row], send_sem=send_sem.at[step], recv_sem=recv_sem.at[step],
            device_id=at_row(step), device_id_type=MESH)

    for step in range(1, rows):
        to_rows(step, bests, send_b, recv_b).start()

    block = (iota(shape, 1) >> 5) == iota(shape, 0)
    for which in range(2):
        whole_rows = moved[which * HIGH:(which + 1) * HIGH]
        placed = jnp.zeros(shape, F32)
        for shift in range(GROUP):
            turned = whole_rows if shift == 0 else pltpu.roll(whole_rows, shift * LOW, 1)
            turned = jnp.where(block, turned, 0.0)
            placed = placed + (turned if shift == 0 else pltpu.roll(turned, GROUP - shift, 0))
        blocks[row, :, which, :] = placed

    for step in range(1, rows):
        to_rows(step, bests, send_b, recv_b).wait()
    every = jnp.concatenate([bests[k] for k in range(rows)], axis=0)
    here = (iota((rows, BINS), 1) & (LOW - 1)) == 0
    top = jnp.max(jnp.where(here, every, -jnp.inf), axis=0, keepdims=True)
    tops_z[z] = jnp.broadcast_to(jnp.max(top, axis=1, keepdims=True), (1, LANES))

    def top_z(step):
        return pltpu.make_async_remote_copy(
            src_ref=tops_z.at[z], dst_ref=tops_z.at[z], send_sem=send_c.at[step], recv_sem=recv_c.at[step],
            device_id=at_z(step), device_id_type=MESH)

    def top_y(step):
        return pltpu.make_async_remote_copy(
            src_ref=tops_y.at[y], dst_ref=tops_y.at[y], send_sem=send_d.at[step], recv_sem=recv_d.at[step],
            device_id=at_y(step), device_id_type=MESH)

    for step in range(1, zs):
        top_z(step).start()
    for step in range(1, rows):
        to_rows(step, blocks, send_e, recv_e).start()
    split = jnp.concatenate([piece.astype(F32) for piece in pieces(every)] + [jnp.zeros((rows, BINS), F32)], axis=0)
    pltpu.matmul_push_rhs(matrices[3], 0, 0)
    pltpu.matmul_acc_lhs(small[3], split.astype(BF16), load_staged_rhs=0)
    full = pltpu.matmul_pop(small[3])
    chosen = full[0:rows] + (full[rows:2 * rows] + full[2 * rows:3 * rows])
    owned = (iota((rows, BINS), 1) >> 3) == iota((rows, BINS), 0)
    line = jnp.sum(jnp.where(owned, chosen, 0.0), axis=0, keepdims=True)
    for step in range(1, zs):
        top_z(step).wait()
    tops_y[y] = jnp.max(tops_z[...], axis=0)
    for step in range(1, ys):
        top_y(step).start()
    for step in range(1, rows):
        to_rows(step, blocks, send_e, recv_e).wait()
    for k in range(rows):
        hist_ref[k * GROUP:(k + 1) * GROUP] = blocks[k]
    for group in range(groups):
        @pl.when(row != group)
        def _():
            scatter(group).wait_send()
    for step in range(1, ys):
        top_y(step).wait()
    largest = jnp.max(tops_y[...], axis=0)
    gain_ref[...] = (line[:, :LANES] / (largest + 1e-6))[:, :rows * GROUP]


def one_round(rows, ys, zs, tiles, scores, labels, ranks, codes):
    vmem = pl.BlockSpec(memory_space=pltpu.VMEM)
    hbm = pl.BlockSpec(memory_space=pltpu.HBM)
    here, docs = codes.shape
    groups = here // GROUP
    feats = ys * zs
    block = pltpu.VMEM((8, LANES), F32)
    dma = pltpu.SemaphoreType.DMA
    pair = lambda n: [dma((n,)), dma((n,))]
    return pl.pallas_call(
        functools.partial(round_kernel, rows, ys, zs),
        out_shape=(block, block, pltpu.VMEM((here, 2, BINS), F32), pltpu.VMEM((1, here), F32)),
        in_specs=[hbm] * 5,
        out_specs=(vmem,) * 4,
        scratch_shapes=[
            pltpu.SMEM((1, QUERIES), jnp.int32), pltpu.VMEM((8, LANES), F32), pltpu.VMEM((8, LANES), jnp.int32),
            pltpu.VMEM((8, LANES), jnp.int32), pltpu.VMEM((here, docs), jnp.int32),
            pltpu.VMEM((3, 24, LANES), F32), pltpu.VMEM((3, 24, LANES, LANES), F32), pltpu.VMEM((feats, 16, LANES), BF16),
            pltpu.VMEM((2, 16, 1024), BF16), pltpu.VMEM((4, BINS, BINS), BF16),
            pltpu.VMEM((groups, 2 * HIGH, BINS), F32), pltpu.VMEM((rows, 2 * HIGH, BINS), F32),
            pltpu.VMEM((rows, GROUP, 2, BINS), F32), pltpu.VMEM((rows, 1, BINS), F32),
            pltpu.VMEM((zs, 1, LANES), F32), pltpu.VMEM((ys, 1, LANES), F32),
            dma((4,)), dma((groups,)), *pair(2), *pair(zs), *pair(ys),
            *pair(rows), *pair(rows), *pair(zs), *pair(ys), *pair(rows),
        ],
        compiler_params=pltpu.CompilerParams(collective_id=0, has_side_effects=True, vmem_limit_bytes=60 * 2 ** 20),
        name="round",
    )(tiles, scores, labels, ranks, codes)


def publish_kernel(*refs):
    sems = refs[-1]
    half = (len(refs) - 1) // 2
    copies = [pltpu.make_async_copy(refs[k], refs[half + k], sems.at[k]) for k in range(half)]
    for copy in copies:
        copy.start()
    for copy in copies:
        copy.wait()


def publish(arrays):
    hbm = pl.BlockSpec(memory_space=pltpu.HBM)
    return pl.pallas_call(
        publish_kernel,
        out_shape=tuple(jax.ShapeDtypeStruct(x.shape, x.dtype) for x in arrays),
        in_specs=[pl.BlockSpec(memory_space=pltpu.VMEM)] * len(arrays),
        out_specs=(hbm,) * len(arrays),
        scratch_shapes=[pltpu.SemaphoreType.DMA((len(arrays),))],
        name="publish",
    )(*[pltpu.with_memory_space_constraint(x, pltpu.VMEM) for x in arrays])


def shards(rows, ys, zs, doc_scores, doc_labels, doc_ranks, query_tiles, bin_codes):
    tile_of = lambda x: x.reshape(8, LANES)
    gradient, hessian, histogram, split_gain = one_round(
        rows, ys, zs, query_tiles, tile_of(doc_scores), tile_of(doc_labels), tile_of(doc_ranks), bin_codes)
    gradient, hessian, histogram, split_gain = publish((gradient, hessian, histogram, split_gain))
    return gradient.reshape(-1), hessian.reshape(-1), histogram, split_gain.reshape(-1)


def solution(mesh):
    return jax.shard_map(
        functools.partial(shards, mesh.shape["row"], 4, mesh.shape["feat"] // 4),
        mesh=mesh,
        in_specs=(P(("row", "feat")), P(("row", "feat")), P(("row", "feat")), P("row", None), P("feat", "row")),
        out_specs=(P(("row", "feat")), P(("row", "feat")), P("feat", None, None), P("feat")),
        check_vma=False,
    )
```

```python
import functools

import jax
import jax.experimental.pallas as pl
import jax.experimental.pallas.tpu as pltpu
import jax.numpy as jnp
from jax import lax
from jax.sharding import PartitionSpec as P

BINS = 256
MAX_TILES = 8
LANES = 128
QUERIES = 64
HIGH, LOW = 8, 32
GROUP = 8
MESH = pl.DeviceIdType.MESH
F32, BF16, F8, I8 = jnp.float32, jnp.bfloat16, jnp.float8_e4m3fn, jnp.int8


def iota(shape, dim):
    return lax.broadcasted_iota(jnp.int32, shape, dim)


def pieces(x):
    first = x.astype(BF16)
    rest = x - first.astype(F32)
    second = rest.astype(BF16)
    third = (rest - second.astype(F32)).astype(BF16)
    return first, second, third


def query_spans(tiles_ref, me):
    first = [jnp.int32(0)] * 8
    count = [jnp.int32(1)] * 8
    start = 8 - me * 8
    for query in range(QUERIES):
        tiles = tiles_ref[0, query]
        for tile in range(8):
            inside = start <= 8 + tile
            first[tile] = jnp.where(inside, start, first[tile])
            count[tile] = jnp.where(inside, tiles, count[tile])
        start = start + tiles
    return first, count


def discount_table():
    place = (iota((8, LANES), 0) * LANES + iota((8, LANES), 1)).astype(F32)
    return place, 1.0 / jnp.log2(place + 2.0)


def query_scale(window, first, count):
    place, table = discount_table()
    rows = iota((8, LANES), 0)
    first_rows, count_rows = jnp.zeros((8, LANES), jnp.int32), jnp.zeros((8, LANES), jnp.int32)
    for tile in range(8):
        first_rows = jnp.where(rows == tile, first[tile], first_rows)
        count_rows = jnp.where(rows == tile, count[tile], count_rows)
    all_gains = window[1]
    reach = jnp.concatenate([(all_gains >= F32(2 ** level - 1)).astype(F32) for level in range(1, 5)], axis=0)
    reach = jnp.broadcast_to(jnp.sum(reach, axis=1, keepdims=True), (96, LANES))
    above = [jnp.zeros((8, LANES), F32)] * 4
    for tile in range(24):
        member = (first_rows <= tile) & (first_rows + count_rows > tile)
        for level in range(4):
            at = level * 24 + tile
            above[level] = above[level] + jnp.where(member, jnp.broadcast_to(reach[at:at + 1], (8, LANES)), 0.0)
    ideals = []
    for tile in range(8):
        total = jnp.zeros((8, LANES), F32)
        for level in range(4):
            limit = jnp.broadcast_to(above[level][tile:tile + 1], (8, LANES))
            total = total + jnp.where(place < limit, table * F32(2 ** level), 0.0)
        ideals.append(jnp.sum(total, axis=0, keepdims=True))
    ideal = jnp.sum(jnp.concatenate(ideals, axis=0), axis=1, keepdims=True)
    return 1.0 / (1.0 + ideal)


def widen(window, wide, slot):
    for which in range(3):
        turned = jnp.transpose(window[which, slot * 8:slot * 8 + 8, :])
        for tile in range(8):
            wide[which, slot * 8 + tile] = jnp.broadcast_to(turned[:, tile:tile + 1], (LANES, LANES))


def pair_sums(own, wide, first, count):
    odds, gains, discs = own
    grads, hessians = [], []
    rows = 32
    for tile in range(8):
        odds_i, gain_i, disc_i = (jnp.broadcast_to(x[tile:tile + 1], (rows, LANES)) for x in own)

        def column(step, carried):
            at = jnp.where(step < count[tile], jnp.minimum(jnp.maximum(first[tile] + step, 0), 23), 24)
            grad, hess = carried
            for part in range(0, LANES, rows):
                odds_j, gain_j, disc_j = (wide[which, at, part:part + rows, :] for which in range(3))
                inverse = pl.reciprocal(odds_i + odds_j, approx=True)
                delta = gain_i - gain_j
                weight = delta * (jnp.abs(disc_i - disc_j) * inverse)
                grad = grad + weight * jnp.where(delta > 0, odds_j, odds_i)
                hess = hess + jnp.abs(weight) * (inverse * odds_j)
            return grad, hess

        empty = jnp.zeros((rows, LANES), F32)
        grad, hess = lax.fori_loop(0, MAX_TILES, column, (empty, empty))
        grads.append(jnp.sum(grad, axis=0, keepdims=True))
        hessians.append(jnp.sum(hess, axis=0, keepdims=True))
    return jnp.concatenate(grads, axis=0), jnp.concatenate(hessians, axis=0)


def build_matrices(matrices):
    source, target = iota((BINS, BINS), 0), iota((BINS, BINS), 1)
    source_low, source_feat = source >> 3, source & 7
    target_feat, target_low = target >> 5, target & 31
    same = source_feat == target_feat
    for k, flag in enumerate((same & (source_low == target_low), same & (source_low <= target_low), same)):
        matrices[k] = jnp.where(flag, F32(1), F32(0)).astype(BF16)
    pick = ((source & (LOW - 1)) == 0) & ((source >> 5) == (target & 7))
    matrices[3] = jnp.where(pick, F32(1), F32(0)).astype(BF16)


def round_kernel(rows, ys, zs, *refs):
    accumulators = ([pltpu.ACC(k % 2)((2 * HIGH * GROUP, BINS), F32) for k in range(rows)]
                    + [pltpu.ACC(k % 2)((48, BINS), F32) for k in range(3)] + [pltpu.ACC(0)((32, BINS), F32)])
    pl.run_scoped(lambda *accs: round_body(rows, ys, zs, accs[:rows], accs[rows:], *refs), *accumulators)


def round_body(rows, ys, zs, accs, small, tiles_hbm, score_hbm, label_hbm, rank_hbm, codes_hbm,
                 grad_ref, hess_ref, hist_ref, gain_ref,
                 tiles_ref, score_ref, label_ref, rank_ref, codes,
                 window, wide, gathered, spread, matrices, mine, parts, blocks, bests, tops,
                 in_sem, code_sem, halo_send, halo_recv, send_z, recv_z, send_y, recv_y,
                 send_a, recv_a, send_b, recv_b, send_c, recv_c, send_e, recv_e):
    row, feat = lax.axis_index("row"), lax.axis_index("feat")
    feats = ys * zs
    y, z = feat // zs, lax.rem(feat, zs)
    groups = codes.shape[0] // GROUP
    chunks = codes.shape[1] // 1024

    loads = [pltpu.make_async_copy(src, dst, in_sem.at[k]) for k, (src, dst) in enumerate(
        ((score_hbm, score_ref), (label_hbm, label_ref), (rank_hbm, rank_ref), (tiles_hbm, tiles_ref)))]
    for load in loads:
        load.start()
    y_low, y_high = lax.rem(y, 2), y // 2

    def y_block(step):
        return lax.rem(y_high + step // 2, 2) * 2 + lax.rem(y_low + step % 2, 2)

    def code_load(step):
        docs = pl.ds(pl.multiple_of(y_block(step) * (zs * 1024), zs * 1024), zs * 1024)
        return pltpu.make_async_copy(codes_hbm.at[:, docs], codes.at[:, docs], code_sem.at[step])


    barrier = pltpu.get_barrier_semaphore()

    def at_row(step):
        return {"row": lax.rem(row + step, rows)}

    def at_z(step):
        return {"feat": y * zs + lax.rem(z + step, zs)}

    def at_y(step):
        return {"feat": y_block(step) * zs + z}

    def at_row_y(step):
        return {"row": lax.rem(row + step // 2, rows), "feat": y_block(step % 2) * zs + z}

    def at_z_y(step):
        return {"feat": y_block(step % 2 * 2) * zs + lax.rem(z + step // 2, zs)}

    def at_feat(step):
        return {"feat": lax.rem(feat + step, feats)}

    def signal(device):
        pl.semaphore_signal(barrier, inc=1, device_id=device, device_id_type=MESH)

    signal(at_feat(1))
    signal(at_feat(feats - 1))
    for step in range(1, 2 * zs):
        signal(at_z_y(step))
    signal(at_y(3))
    for step in range(1, 2 * rows):
        signal(at_row_y(step))
    for load in loads:
        load.wait()

    odds = jnp.exp(score_ref[...])
    gains = (jnp.left_shift(1, label_ref[...]) - 1).astype(F32)
    discs = 1.0 / jnp.log2(rank_ref[...].astype(F32) + 2.0)
    own = (odds, gains, discs)
    for which in range(3):
        window[which, 8:16, :] = own[which]
    for which, value in enumerate((0.0, -1.0, 0.0)):
        wide[which, 24] = jnp.full((LANES, LANES), value, F32)
    build_matrices(matrices)
    pl.semaphore_wait(barrier, 2 + 2 * zs - 1 + 1 + 2 * rows - 1)
    halos = []
    for side, (target, place) in enumerate(((feats - 1, 16), (1, 0))):
        copy = pltpu.make_async_remote_copy(
            src_ref=window.at[:, pl.ds(8, 8), :], dst_ref=window.at[:, pl.ds(place, 8), :],
            send_sem=halo_send.at[side], recv_sem=halo_recv.at[side],
            device_id=at_feat(target), device_id_type=MESH)
        copy.start()
        halos.append(copy)
    code_load(0).start()
    first, count = query_spans(tiles_ref, feat)
    widen(window, wide, 1)
    for copy in halos:
        copy.wait()
    for step in range(1, ys):
        code_load(step).start()
    widen(window, wide, 0)
    widen(window, wide, 2)
    scale = query_scale(window, first, count)
    grad, hess = pair_sums(own, wide, first, count)
    grad = -grad * scale
    hess = hess * (odds * scale)
    grad_ref[...] = grad
    hess_ref[...] = hess
    gathered[feat] = jnp.concatenate([grad, hess], axis=0).astype(BF16)

    def over_z(step):
        return pltpu.make_async_remote_copy(
            src_ref=gathered.at[feat], dst_ref=gathered.at[feat], send_sem=send_z.at[step], recv_sem=recv_z.at[step],
            device_id=at_z(step), device_id_type=MESH)

    def over_y(step):
        block = gathered.at[pl.ds(y * zs, zs)]
        return pltpu.make_async_remote_copy(
            src_ref=block, dst_ref=block, send_sem=send_y.at[step], recv_sem=recv_y.at[step],
            device_id=at_y(step), device_id_type=MESH)

    offsets = [(turn + 1) // 2 if turn % 2 else zs - turn // 2 for turn in range(1, zs)]
    for step in offsets:
        over_z(step).start()
    code_load(0).wait()

    def scatter(group):
        return pltpu.make_async_remote_copy(
            src_ref=mine.at[group], dst_ref=parts.at[row], send_sem=send_a.at[group], recv_sem=recv_a.at[row],
            device_id={"row": jnp.int32(group)}, device_id_type=MESH)

    def arrival(step):
        source = lax.rem(row + step, rows)
        return pltpu.make_async_remote_copy(
            src_ref=parts.at[source], dst_ref=parts.at[source], send_sem=send_a.at[source], recv_sem=recv_a.at[source],
            device_id=at_row(step), device_id_type=MESH)

    zero = jnp.zeros((), BF16)

    @pl.loop(0, chunks)
    def _(turn):
        for at in range(1, 5):
            @pl.when(turn == at)
            def _():
                for offset in offsets[at - 1:at] if at < 4 else offsets[at - 1:]:
                    over_z(zs - offset).wait_recv()
                if at == 4:
                    for step in range(1, ys):
                        over_y(step).start()

        for step in range(1, ys):
            @pl.when(turn == step * zs)
            def _():
                over_y(step).wait_recv()
                code_load(step).wait()

        inner = lax.rem(turn, zs)
        odd = lax.rem(inner, 2)
        offset = odd * ((inner + 1) // 2) + (1 - odd) * (zs - inner // 2)
        outer = turn // zs
        owner_y = lax.rem(y_high + outer // 2, 2) * 2 + lax.rem(y_low + lax.rem(outer, 2), 2)
        owner = owner_y * zs + lax.rem(z + offset, zs)
        part = gathered[owner].astype(F32)
        for which in range(2):
            for tile in range(8):
                line = which * 8 + tile
                spread[which, :, tile * LANES:(tile + 1) * LANES] = jnp.broadcast_to(
                    part[line:line + 1], (16, LANES)).astype(BF16)
        for k in range(1024 // BINS):
            at = pl.ds(pl.multiple_of(owner * 1024 + k * BINS, BINS), BINS)
            lam = [spread[which, :, k * BINS:(k + 1) * BINS] for which in range(2)]
            for group in range(groups):
                code = codes[group * GROUP:(group + 1) * GROUP, at]
                high = (code >> 5).astype(F32)
                high = jnp.concatenate([high, high - 1.0], axis=0).astype(BF16)
                hits = [high == jnp.array(2 * k, BF16) for k in range(HIGH // 2)]
                lhs = jnp.concatenate([jnp.where(hit, value, zero) for value in lam for hit in hits], axis=0)
                low = code & (LOW - 1)
                low = jnp.concatenate([low - k for k in range(4)], axis=0).astype(I8)
                rhs = jnp.concatenate(
                    [jnp.where(low == jnp.array(4 * k, I8), jnp.ones((), F8), jnp.zeros((), F8))
                     for k in range(LOW // 4)], axis=0)
                stage = group // 2 % 2
                pltpu.matmul_push_rhs(rhs, stage, group % 2, transpose=True)
                pltpu.matmul_acc_lhs(accs[group], lhs, load_staged_rhs=stage)

    shape = (2 * HIGH, GROUP, BINS)
    same = iota(shape, 1) == (iota(shape, 2) & (GROUP - 1))
    for group in range(groups):
        total = pltpu.matmul_pop(accs[group]).reshape(shape)
        mine[group] = jnp.sum(jnp.where(same, total, 0.0), axis=1)

        @pl.when(row != group)
        def _():
            scatter(group).start()


    for step in range(1, zs):
        over_z(step).wait_send()
    for step in range(1, ys):
        over_y(step).wait_send()
    parts[row] = mine[row]
    for step in range(1, rows):
        arrival(step).wait_recv()
    summed = parts[0]
    for k in range(1, rows):
        summed = summed + parts[k]

    split = jnp.concatenate(pieces(summed), axis=0)
    for k in range(3):
        pltpu.matmul_push_rhs(matrices[k], k // 2, k % 2)
        pltpu.matmul_acc_lhs(small[k], split, load_staged_rhs=k // 2)

    def product(k):
        full = pltpu.matmul_pop(small[k])
        return full[0:16] + (full[16:32] + full[32:48])

    left, across, moved = product(1), product(2), product(0)
    running = [jnp.zeros((1, BINS), F32)] * 2
    sides = [[], []]
    for which in range(2):
        for k in range(HIGH):
            at = which * HIGH + k
            sides[which].append(left[at:at + 1] + running[which])
            running[which] = running[which] + across[at:at + 1]
    grad_left, hess_left = (jnp.concatenate(side, axis=0) for side in sides)
    grad_all, hess_all = running
    grad_right = grad_all - grad_left
    gain = (grad_left * grad_left / (hess_left + 1.0)
            + grad_right * grad_right / (hess_all - hess_left + 1.0)
            - grad_all * grad_all / (hess_all + 1.0))
    shape = (HIGH, BINS)
    last = (iota(shape, 0) == HIGH - 1) & ((iota(shape, 1) & (LOW - 1)) == LOW - 1)
    gain = jnp.where(last, -jnp.inf, gain)
    place_a = row * 2 + y_low
    bests[place_a] = jnp.max(gain, axis=0, keepdims=True)

    def send_best(step):
        return pltpu.make_async_remote_copy(
            src_ref=bests.at[place_a], dst_ref=bests.at[place_a], send_sem=send_b.at[step], recv_sem=recv_b.at[step],
            device_id=at_row_y(step), device_id_type=MESH)

    for step in range(1, 2 * rows):
        send_best(step).start()

    def send_block(step):
        return pltpu.make_async_remote_copy(
            src_ref=blocks.at[row], dst_ref=blocks.at[row], send_sem=send_e.at[step], recv_sem=recv_e.at[step],
            device_id=at_row(step), device_id_type=MESH)

    block = (iota(shape, 1) >> 5) == iota(shape, 0)
    for which in range(2):
        whole_rows = moved[which * HIGH:(which + 1) * HIGH]
        placed = jnp.zeros(shape, F32)
        for shift in range(GROUP):
            turned = whole_rows if shift == 0 else pltpu.roll(whole_rows, shift * LOW, 1)
            turned = jnp.where(block, turned, 0.0)
            placed = placed + (turned if shift == 0 else pltpu.roll(turned, GROUP - shift, 0))
        blocks[row, :, which, :] = placed

    for step in range(1, 2 * rows):
        send_best(step).wait()
    top = jnp.max(bests[...], axis=0)
    place_b = z * 2 + y_high
    tops[place_b] = jnp.broadcast_to(jnp.max(top, axis=1, keepdims=True), (1, LANES))

    def send_top(step):
        return pltpu.make_async_remote_copy(
            src_ref=tops.at[place_b], dst_ref=tops.at[place_b], send_sem=send_c.at[step], recv_sem=recv_c.at[step],
            device_id=at_z_y(step), device_id_type=MESH)

    for step in range(1, 2 * zs):
        send_top(step).start()
    for step in range(1, rows):
        send_block(step).start()
    every = jnp.concatenate([bests[k * 2 + y_low] for k in range(rows)], axis=0)
    for shift in (1, 2, 4, 8, 16):
        every = jnp.maximum(every, pltpu.roll(every, BINS - shift, 1))
    every = jnp.where((iota((rows, BINS), 1) & (LOW - 1)) == 0, every, 0.0)
    split = jnp.concatenate([piece.astype(F32) for piece in pieces(every)] + [jnp.zeros((rows, BINS), F32)], axis=0)
    pltpu.matmul_push_rhs(matrices[3], 0, 0)
    pltpu.matmul_acc_lhs(small[3], split.astype(BF16), load_staged_rhs=0)
    full = pltpu.matmul_pop(small[3])
    chosen = full[0:rows] + (full[rows:2 * rows] + full[2 * rows:3 * rows])
    owned = (iota((rows, BINS), 1) >> 3) == iota((rows, BINS), 0)
    line = jnp.sum(jnp.where(owned, chosen, 0.0), axis=0, keepdims=True)
    for step in range(1, rows):
        send_block(step).wait()
    for k in range(rows):
        hist_ref[k * GROUP:(k + 1) * GROUP] = blocks[k]
    for group in range(groups):
        @pl.when(row != group)
        def _():
            scatter(group).wait_send()
    for step in range(1, 2 * zs):
        send_top(step).wait()
    largest = jnp.max(tops[...], axis=0)
    gain_ref[...] = (line[:, :LANES] / (largest + 1e-6))[:, :rows * GROUP]


def one_round(rows, ys, zs, tiles, scores, labels, ranks, codes):
    vmem = pl.BlockSpec(memory_space=pltpu.VMEM)
    hbm = pl.BlockSpec(memory_space=pltpu.HBM)
    here, docs = codes.shape
    groups = here // GROUP
    feats = ys * zs
    block = pltpu.VMEM((8, LANES), F32)
    dma = pltpu.SemaphoreType.DMA
    pair = lambda n: [dma((n,)), dma((n,))]
    return pl.pallas_call(
        functools.partial(round_kernel, rows, ys, zs),
        out_shape=(block, block, pltpu.VMEM((here, 2, BINS), F32), pltpu.VMEM((1, here), F32)),
        in_specs=[hbm] * 5,
        out_specs=(vmem,) * 4,
        scratch_shapes=[
            pltpu.SMEM((1, QUERIES), jnp.int32), pltpu.VMEM((8, LANES), F32), pltpu.VMEM((8, LANES), jnp.int32),
            pltpu.VMEM((8, LANES), jnp.int32), pltpu.VMEM((here, docs), jnp.int32),
            pltpu.VMEM((3, 24, LANES), F32), pltpu.VMEM((3, 25, LANES, LANES), F32), pltpu.VMEM((feats, 16, LANES), BF16),
            pltpu.VMEM((2, 16, 1024), BF16), pltpu.VMEM((4, BINS, BINS), BF16),
            pltpu.VMEM((groups, 2 * HIGH, BINS), F32), pltpu.VMEM((rows, 2 * HIGH, BINS), F32),
            pltpu.VMEM((rows, GROUP, 2, BINS), F32), pltpu.VMEM((2 * rows, 1, BINS), F32),
            pltpu.VMEM((2 * zs, 1, LANES), F32),
            dma((4,)), dma((ys,)), *pair(2), *pair(zs), *pair(ys),
            *pair(rows), *pair(2 * rows), *pair(2 * zs), *pair(rows),
        ],
        compiler_params=pltpu.CompilerParams(collective_id=0, has_side_effects=True, vmem_limit_bytes=60 * 2 ** 20),
        name="round",
    )(tiles, scores, labels, ranks, codes)


def publish_kernel(*refs):
    sems = refs[-1]
    half = (len(refs) - 1) // 2
    copies = [pltpu.make_async_copy(refs[k], refs[half + k], sems.at[k]) for k in range(half)]
    for copy in copies:
        copy.start()
    for copy in copies:
        copy.wait()


def publish(arrays):
    hbm = pl.BlockSpec(memory_space=pltpu.HBM)
    return pl.pallas_call(
        publish_kernel,
        out_shape=tuple(jax.ShapeDtypeStruct(x.shape, x.dtype) for x in arrays),
        in_specs=[pl.BlockSpec(memory_space=pltpu.VMEM)] * len(arrays),
        out_specs=(hbm,) * len(arrays),
        scratch_shapes=[pltpu.SemaphoreType.DMA((len(arrays),))],
        name="publish",
    )(*[pltpu.with_memory_space_constraint(x, pltpu.VMEM) for x in arrays])


def shards(rows, ys, zs, doc_scores, doc_labels, doc_ranks, query_tiles, bin_codes):
    tile_of = lambda x: x.reshape(8, LANES)
    gradient, hessian, histogram, split_gain = one_round(
        rows, ys, zs, query_tiles, tile_of(doc_scores), tile_of(doc_labels), tile_of(doc_ranks), bin_codes)
    gradient, hessian, histogram, split_gain = publish((gradient, hessian, histogram, split_gain))
    return gradient.reshape(-1), hessian.reshape(-1), histogram, split_gain.reshape(-1)


def solution(mesh):
    return jax.shard_map(
        functools.partial(shards, mesh.shape["row"], 4, mesh.shape["feat"] // 4),
        mesh=mesh,
        in_specs=(P(("row", "feat")), P(("row", "feat")), P(("row", "feat")), P("row", None), P("feat", "row")),
        out_specs=(P(("row", "feat")), P(("row", "feat")), P("feat", None, None), P("feat")),
        check_vma=False,
    )
```

```python
import functools

import jax
import jax.experimental.pallas as pl
import jax.experimental.pallas.tpu as pltpu
import jax.numpy as jnp
from jax import lax
from jax.sharding import PartitionSpec as P

BINS = 256
MAX_TILES = 8
LANES = 128
QUERIES = 64
HIGH, LOW = 8, 32
GROUP = 8
MESH = pl.DeviceIdType.MESH
F32, BF16, F8, I8 = jnp.float32, jnp.bfloat16, jnp.float8_e4m3fn, jnp.int8


def iota(shape, dim):
    return lax.broadcasted_iota(jnp.int32, shape, dim)


def pieces(x):
    first = x.astype(BF16)
    rest = x - first.astype(F32)
    second = rest.astype(BF16)
    third = (rest - second.astype(F32)).astype(BF16)
    return first, second, third


def query_spans(tiles_ref, me):
    first = [jnp.int32(0)] * 8
    count = [jnp.int32(1)] * 8
    start = 8 - me * 8
    for query in range(QUERIES):
        tiles = tiles_ref[0, query]
        for tile in range(8):
            inside = start <= 8 + tile
            first[tile] = jnp.where(inside, start, first[tile])
            count[tile] = jnp.where(inside, tiles, count[tile])
        start = start + tiles
    return first, count


def discount_table():
    place = (iota((8, LANES), 0) * LANES + iota((8, LANES), 1)).astype(F32)
    return place, 1.0 / jnp.log2(place + 2.0)


def query_scale(window, first, count):
    place, table = discount_table()
    rows = iota((8, LANES), 0)
    first_rows, count_rows = jnp.zeros((8, LANES), jnp.int32), jnp.zeros((8, LANES), jnp.int32)
    for tile in range(8):
        first_rows = jnp.where(rows == tile, first[tile], first_rows)
        count_rows = jnp.where(rows == tile, count[tile], count_rows)
    all_gains = window[1]
    reach = jnp.concatenate([(all_gains >= F32(2 ** level - 1)).astype(F32) for level in range(1, 5)], axis=0)
    reach = jnp.broadcast_to(jnp.sum(reach, axis=1, keepdims=True), (96, LANES))
    above = [jnp.zeros((8, LANES), F32)] * 4
    for tile in range(24):
        member = (first_rows <= tile) & (first_rows + count_rows > tile)
        for level in range(4):
            at = level * 24 + tile
            above[level] = above[level] + jnp.where(member, jnp.broadcast_to(reach[at:at + 1], (8, LANES)), 0.0)
    ideals = []
    for tile in range(8):
        total = jnp.zeros((8, LANES), F32)
        for level in range(4):
            limit = jnp.broadcast_to(above[level][tile:tile + 1], (8, LANES))
            total = total + jnp.where(place < limit, table * F32(2 ** level), 0.0)
        ideals.append(jnp.sum(total, axis=0, keepdims=True))
    ideal = jnp.sum(jnp.concatenate(ideals, axis=0), axis=1, keepdims=True)
    return 1.0 / (1.0 + ideal)


def widen(window, wide, slot):
    for which in range(3):
        turned = jnp.transpose(window[which, slot * 8:slot * 8 + 8, :])
        for tile in range(8):
            wide[which, slot * 8 + tile] = jnp.broadcast_to(turned[:, tile:tile + 1], (LANES, LANES))


def pair_sums(own, wide, first, count):
    odds, gains, discs = own
    grads, hessians = [], []
    rows = 32
    for tile in range(8):
        odds_i, gain_i, disc_i = (jnp.broadcast_to(x[tile:tile + 1], (rows, LANES)) for x in own)

        def column(step, carried):
            at = jnp.where(step < count[tile], jnp.minimum(jnp.maximum(first[tile] + step, 0), 23), 24)
            grad, hess = carried
            for part in range(0, LANES, rows):
                odds_j, gain_j, disc_j = (wide[which, at, part:part + rows, :] for which in range(3))
                inverse = pl.reciprocal(odds_i + odds_j, approx=True)
                delta = gain_i - gain_j
                weight = delta * (jnp.abs(disc_i - disc_j) * inverse)
                grad = grad + weight * jnp.where(delta > 0, odds_j, odds_i)
                hess = hess + jnp.abs(weight) * (inverse * odds_j)
            return grad, hess

        empty = jnp.zeros((rows, LANES), F32)
        grad, hess = lax.fori_loop(0, MAX_TILES, column, (empty, empty))
        grads.append(jnp.sum(grad, axis=0, keepdims=True))
        hessians.append(jnp.sum(hess, axis=0, keepdims=True))
    return jnp.concatenate(grads, axis=0), jnp.concatenate(hessians, axis=0)


def build_matrices(matrices):
    source, target = iota((BINS, BINS), 0), iota((BINS, BINS), 1)
    source_low, source_feat = source >> 3, source & 7
    target_feat, target_low = target >> 5, target & 31
    same = source_feat == target_feat
    for k, flag in enumerate((same & (source_low == target_low), same & (source_low <= target_low), same)):
        matrices[k] = jnp.where(flag, F32(1), F32(0)).astype(BF16)
    pick = ((source & (LOW - 1)) == 0) & ((source >> 5) == (target & 7))
    matrices[3] = jnp.where(pick, F32(1), F32(0)).astype(BF16)


def round_kernel(rows, ys, zs, *refs):
    accumulators = ([pltpu.ACC(k % 2)((2 * HIGH * GROUP, BINS), F32) for k in range(rows)]
                    + [pltpu.ACC(k % 2)((48, BINS), F32) for k in range(3)] + [pltpu.ACC(0)((32, BINS), F32)])
    pl.run_scoped(lambda *accs: round_body(rows, ys, zs, accs[:rows], accs[rows:], *refs), *accumulators)


def round_body(rows, ys, zs, accs, small, tiles_hbm, score_hbm, label_hbm, rank_hbm, codes_hbm,
                 grad_ref, hess_ref, hist_ref, gain_ref,
                 tiles_ref, score_ref, label_ref, rank_ref, codes,
                 window, wide, gathered, spread, matrices, mine, parts, blocks, bests, tops,
                 in_sem, code_sem, halo_send, halo_recv, send_z, recv_z, send_y, recv_y,
                 send_a, recv_a, send_b, recv_b, send_c, recv_c, send_e, recv_e):
    row, feat = lax.axis_index("row"), lax.axis_index("feat")
    feats = ys * zs
    y, z = feat // zs, lax.rem(feat, zs)
    groups = codes.shape[0] // GROUP
    chunks = codes.shape[1] // 1024

    loads = [pltpu.make_async_copy(src, dst, in_sem.at[k]) for k, (src, dst) in enumerate(
        ((score_hbm, score_ref), (label_hbm, label_ref), (rank_hbm, rank_ref), (tiles_hbm, tiles_ref)))]
    for load in loads:
        load.start()
    y_low, y_high = lax.rem(y, 2), y // 2

    def y_block(step):
        return lax.rem(y_high + step // 2, 2) * 2 + lax.rem(y_low + step % 2, 2)

    def code_load(step):
        docs = pl.ds(pl.multiple_of(y_block(step) * (zs * 1024), zs * 1024), zs * 1024)
        return pltpu.make_async_copy(codes_hbm.at[:, docs], codes.at[:, docs], code_sem.at[step])


    barrier = pltpu.get_barrier_semaphore()

    def at_row(step):
        return {"row": lax.rem(row + step, rows)}

    def at_z(step):
        return {"feat": y * zs + lax.rem(z + step, zs)}

    def at_y(step):
        return {"feat": y_block(step) * zs + z}

    def at_row_y(step):
        return {"row": lax.rem(row + step // 2, rows), "feat": y_block(step % 2) * zs + z}

    def at_z_y(step):
        return {"feat": y_block(step % 2 * 2) * zs + lax.rem(z + step // 2, zs)}

    def at_feat(step):
        return {"feat": lax.rem(feat + step, feats)}

    def signal(device):
        pl.semaphore_signal(barrier, inc=1, device_id=device, device_id_type=MESH)

    signal(at_feat(1))
    signal(at_feat(feats - 1))
    for step in range(1, 2 * zs):
        signal(at_z_y(step))
    signal(at_y(3))
    for step in range(1, 2 * rows):
        signal(at_row_y(step))
    for load in loads:
        load.wait()

    odds = jnp.exp(score_ref[...])
    gains = (jnp.left_shift(1, label_ref[...]) - 1).astype(F32)
    discs = 1.0 / jnp.log2(rank_ref[...].astype(F32) + 2.0)
    own = (odds, gains, discs)
    for which in range(3):
        window[which, 8:16, :] = own[which]
    pl.semaphore_wait(barrier, 2 + 2 * zs - 1 + 1 + 2 * rows - 1)
    halos = []
    for side, (target, place) in enumerate(((feats - 1, 16), (1, 0))):
        copy = pltpu.make_async_remote_copy(
            src_ref=window.at[:, pl.ds(8, 8), :], dst_ref=window.at[:, pl.ds(place, 8), :],
            send_sem=halo_send.at[side], recv_sem=halo_recv.at[side],
            device_id=at_feat(target), device_id_type=MESH)
        copy.start()
        halos.append(copy)
    code_load(0).start()
    for which, value in enumerate((0.0, -1.0, 0.0)):
        wide[which, 24] = jnp.full((LANES, LANES), value, F32)
    build_matrices(matrices)
    first, count = query_spans(tiles_ref, feat)
    widen(window, wide, 1)
    for copy in halos:
        copy.wait()
    for step in range(1, ys):
        code_load(step).start()
    widen(window, wide, 0)
    widen(window, wide, 2)
    scale = query_scale(window, first, count)
    grad, hess = pair_sums(own, wide, first, count)
    grad = -grad * scale
    hess = hess * (odds * scale)
    grad_ref[...] = grad
    hess_ref[...] = hess
    gathered[feat] = jnp.concatenate([grad, hess], axis=0).astype(BF16)

    def over_z(step):
        return pltpu.make_async_remote_copy(
            src_ref=gathered.at[feat], dst_ref=gathered.at[feat], send_sem=send_z.at[step], recv_sem=recv_z.at[step],
            device_id=at_z(step), device_id_type=MESH)

    def over_y(step):
        block = gathered.at[pl.ds(y * zs, zs)]
        return pltpu.make_async_remote_copy(
            src_ref=block, dst_ref=block, send_sem=send_y.at[step], recv_sem=recv_y.at[step],
            device_id=at_y(step), device_id_type=MESH)

    offsets = [(turn + 1) // 2 if turn % 2 else zs - turn // 2 for turn in range(1, zs)]
    for step in offsets:
        over_z(step).start()
    code_load(0).wait()

    def scatter(group):
        return pltpu.make_async_remote_copy(
            src_ref=mine.at[group], dst_ref=parts.at[row], send_sem=send_a.at[group], recv_sem=recv_a.at[row],
            device_id={"row": jnp.int32(group)}, device_id_type=MESH)

    def arrival(step):
        source = lax.rem(row + step, rows)
        return pltpu.make_async_remote_copy(
            src_ref=parts.at[source], dst_ref=parts.at[source], send_sem=send_a.at[source], recv_sem=recv_a.at[source],
            device_id=at_row(step), device_id_type=MESH)

    zero = jnp.zeros((), BF16)

    def arrived(offset):
        over_z(zs - offset).wait_recv()

    def owner_of(turn):
        inner = lax.rem(turn, zs)
        odd = lax.rem(inner, 2)
        offset = odd * ((inner + 1) // 2) + (1 - odd) * (zs - inner // 2)
        outer = turn // zs
        owner_y = lax.rem(y_high + outer // 2, 2) * 2 + lax.rem(y_low + lax.rem(outer, 2), 2)
        return owner_y * zs + lax.rem(z + offset, zs)

    def add_chunks(owners):
        for slot, owner in enumerate(owners):
            part = gathered[owner].astype(F32)
            for which in range(2):
                for tile in range(8):
                    line = which * 8 + tile
                    at = slot * 1024 + tile * LANES
                    spread[which, :, at:at + LANES] = jnp.broadcast_to(part[line:line + 1], (16, LANES)).astype(BF16)
        for slot, owner in enumerate(owners):
            for k in range(1024 // BINS):
                at = pl.ds(pl.multiple_of(owner * 1024 + k * BINS, BINS), BINS)
                there = slot * 1024 + k * BINS
                lam = [spread[which, :, there:there + BINS] for which in range(2)]
                for group in range(groups):
                    code = codes[group * GROUP:(group + 1) * GROUP, at]
                    high = (code >> 5).astype(F32)
                    high = jnp.concatenate([high, high - 1.0], axis=0).astype(BF16)
                    hits = [high == jnp.array(2 * k, BF16) for k in range(HIGH // 2)]
                    lhs = jnp.concatenate([jnp.where(hit, value, zero) for value in lam for hit in hits], axis=0)
                    low = code & (LOW - 1)
                    low = jnp.concatenate([low - k for k in range(4)], axis=0).astype(I8)
                    rhs = jnp.concatenate(
                        [jnp.where(low == jnp.array(4 * k, I8), jnp.ones((), F8), jnp.zeros((), F8))
                         for k in range(LOW // 4)], axis=0)
                    stage = group // 2 % 2
                    pltpu.matmul_push_rhs(rhs, stage, group % 2, transpose=True)
                    pltpu.matmul_acc_lhs(accs[group], lhs, load_staged_rhs=stage)

    @pl.loop(0, 2)
    def _(turn):
        @pl.when(turn == 1)
        def _():
            arrived(offsets[0])

        add_chunks([owner_of(turn)])

    @pl.loop(0, (chunks - 2) // 2)
    def _(pair):
        turn = 2 * pair + 2

        @pl.when(turn == 2)
        def _():
            for offset in offsets[1:3]:
                arrived(offset)

        @pl.when(turn == 4)
        def _():
            for offset in offsets[3:]:
                arrived(offset)
            for step in range(1, ys):
                over_y(step).start()

        for step in range(1, ys):
            @pl.when(turn == step * zs)
            def _():
                over_y(step).wait_recv()
                code_load(step).wait()

        add_chunks([owner_of(turn), owner_of(turn + 1)])

    shape = (2 * HIGH, GROUP, BINS)
    same = iota(shape, 1) == (iota(shape, 2) & (GROUP - 1))
    for group in range(groups):
        total = pltpu.matmul_pop(accs[group]).reshape(shape)
        mine[group] = jnp.sum(jnp.where(same, total, 0.0), axis=1)

        @pl.when(row != group)
        def _():
            scatter(group).start()


    for step in range(1, zs):
        over_z(step).wait_send()
    for step in range(1, ys):
        over_y(step).wait_send()
    parts[row] = mine[row]
    for step in range(1, rows):
        arrival(step).wait_recv()
    summed = parts[0]
    for k in range(1, rows):
        summed = summed + parts[k]

    split = jnp.concatenate(pieces(summed), axis=0)
    for k in range(3):
        pltpu.matmul_push_rhs(matrices[k], k // 2, k % 2)
        pltpu.matmul_acc_lhs(small[k], split, load_staged_rhs=k // 2)

    def product(k):
        full = pltpu.matmul_pop(small[k])
        return full[0:16] + (full[16:32] + full[32:48])

    left, across, moved = product(1), product(2), product(0)
    running = [jnp.zeros((1, BINS), F32)] * 2
    sides = [[], []]
    for which in range(2):
        for k in range(HIGH):
            at = which * HIGH + k
            sides[which].append(left[at:at + 1] + running[which])
            running[which] = running[which] + across[at:at + 1]
    grad_left, hess_left = (jnp.concatenate(side, axis=0) for side in sides)
    grad_all, hess_all = running
    grad_right = grad_all - grad_left
    gain = (grad_left * grad_left / (hess_left + 1.0)
            + grad_right * grad_right / (hess_all - hess_left + 1.0)
            - grad_all * grad_all / (hess_all + 1.0))
    shape = (HIGH, BINS)
    last = (iota(shape, 0) == HIGH - 1) & ((iota(shape, 1) & (LOW - 1)) == LOW - 1)
    gain = jnp.where(last, -jnp.inf, gain)
    place_a = row * 2 + y_low
    bests[place_a] = jnp.max(gain, axis=0, keepdims=True)

    def send_best(step):
        return pltpu.make_async_remote_copy(
            src_ref=bests.at[place_a], dst_ref=bests.at[place_a], send_sem=send_b.at[step], recv_sem=recv_b.at[step],
            device_id=at_row_y(step), device_id_type=MESH)

    for step in range(1, 2 * rows):
        send_best(step).start()

    def send_block(step):
        return pltpu.make_async_remote_copy(
            src_ref=blocks.at[row], dst_ref=blocks.at[row], send_sem=send_e.at[step], recv_sem=recv_e.at[step],
            device_id=at_row(step), device_id_type=MESH)

    block = (iota(shape, 1) >> 5) == iota(shape, 0)
    for which in range(2):
        whole_rows = moved[which * HIGH:(which + 1) * HIGH]
        placed = jnp.zeros(shape, F32)
        for shift in range(GROUP):
            turned = whole_rows if shift == 0 else pltpu.roll(whole_rows, shift * LOW, 1)
            turned = jnp.where(block, turned, 0.0)
            placed = placed + (turned if shift == 0 else pltpu.roll(turned, GROUP - shift, 0))
        blocks[row, :, which, :] = placed

    for step in range(1, 2 * rows):
        send_best(step).wait()
    top = jnp.max(bests[...], axis=0)
    place_b = z * 2 + y_high
    tops[place_b] = jnp.broadcast_to(jnp.max(top, axis=1, keepdims=True), (1, LANES))

    def send_top(step):
        return pltpu.make_async_remote_copy(
            src_ref=tops.at[place_b], dst_ref=tops.at[place_b], send_sem=send_c.at[step], recv_sem=recv_c.at[step],
            device_id=at_z_y(step), device_id_type=MESH)

    for step in range(1, 2 * zs):
        send_top(step).start()
    for step in range(1, rows):
        send_block(step).start()
    every = jnp.concatenate([bests[k * 2 + y_low] for k in range(rows)], axis=0)
    for shift in (1, 2, 4, 8, 16):
        every = jnp.maximum(every, pltpu.roll(every, BINS - shift, 1))
    every = jnp.where((iota((rows, BINS), 1) & (LOW - 1)) == 0, every, 0.0)
    split = jnp.concatenate([piece.astype(F32) for piece in pieces(every)] + [jnp.zeros((rows, BINS), F32)], axis=0)
    pltpu.matmul_push_rhs(matrices[3], 0, 0)
    pltpu.matmul_acc_lhs(small[3], split.astype(BF16), load_staged_rhs=0)
    full = pltpu.matmul_pop(small[3])
    chosen = full[0:rows] + (full[rows:2 * rows] + full[2 * rows:3 * rows])
    owned = (iota((rows, BINS), 1) >> 3) == iota((rows, BINS), 0)
    line = jnp.sum(jnp.where(owned, chosen, 0.0), axis=0, keepdims=True)
    for step in range(1, rows):
        send_block(step).wait()
    for k in range(rows):
        hist_ref[k * GROUP:(k + 1) * GROUP] = blocks[k]
    for group in range(groups):
        @pl.when(row != group)
        def _():
            scatter(group).wait_send()
    for step in range(1, 2 * zs):
        send_top(step).wait()
    largest = jnp.max(tops[...], axis=0)
    gain_ref[...] = (line[:, :LANES] / (largest + 1e-6))[:, :rows * GROUP]


def one_round(rows, ys, zs, tiles, scores, labels, ranks, codes):
    vmem = pl.BlockSpec(memory_space=pltpu.VMEM)
    hbm = pl.BlockSpec(memory_space=pltpu.HBM)
    here, docs = codes.shape
    groups = here // GROUP
    feats = ys * zs
    block = pltpu.VMEM((8, LANES), F32)
    dma = pltpu.SemaphoreType.DMA
    pair = lambda n: [dma((n,)), dma((n,))]
    return pl.pallas_call(
        functools.partial(round_kernel, rows, ys, zs),
        out_shape=(block, block, pltpu.VMEM((here, 2, BINS), F32), pltpu.VMEM((1, here), F32)),
        in_specs=[hbm] * 5,
        out_specs=(vmem,) * 4,
        scratch_shapes=[
            pltpu.SMEM((1, QUERIES), jnp.int32), pltpu.VMEM((8, LANES), F32), pltpu.VMEM((8, LANES), jnp.int32),
            pltpu.VMEM((8, LANES), jnp.int32), pltpu.VMEM((here, docs), jnp.int32),
            pltpu.VMEM((3, 24, LANES), F32), pltpu.VMEM((3, 25, LANES, LANES), F32), pltpu.VMEM((feats, 16, LANES), BF16),
            pltpu.VMEM((2, 16, 2048), BF16), pltpu.VMEM((4, BINS, BINS), BF16),
            pltpu.VMEM((groups, 2 * HIGH, BINS), F32), pltpu.VMEM((rows, 2 * HIGH, BINS), F32),
            pltpu.VMEM((rows, GROUP, 2, BINS), F32), pltpu.VMEM((2 * rows, 1, BINS), F32),
            pltpu.VMEM((2 * zs, 1, LANES), F32),
            dma((4,)), dma((ys,)), *pair(2), *pair(zs), *pair(ys),
            *pair(rows), *pair(2 * rows), *pair(2 * zs), *pair(rows),
        ],
        compiler_params=pltpu.CompilerParams(collective_id=0, has_side_effects=True, vmem_limit_bytes=60 * 2 ** 20),
        name="round",
    )(tiles, scores, labels, ranks, codes)


def publish_kernel(*refs):
    sems = refs[-1]
    half = (len(refs) - 1) // 2
    copies = [pltpu.make_async_copy(refs[k], refs[half + k], sems.at[k]) for k in range(half)]
    for copy in copies:
        copy.start()
    for copy in copies:
        copy.wait()


def publish(arrays):
    hbm = pl.BlockSpec(memory_space=pltpu.HBM)
    return pl.pallas_call(
        publish_kernel,
        out_shape=tuple(jax.ShapeDtypeStruct(x.shape, x.dtype) for x in arrays),
        in_specs=[pl.BlockSpec(memory_space=pltpu.VMEM)] * len(arrays),
        out_specs=(hbm,) * len(arrays),
        scratch_shapes=[pltpu.SemaphoreType.DMA((len(arrays),))],
        name="publish",
    )(*[pltpu.with_memory_space_constraint(x, pltpu.VMEM) for x in arrays])


def shards(rows, ys, zs, doc_scores, doc_labels, doc_ranks, query_tiles, bin_codes):
    tile_of = lambda x: x.reshape(8, LANES)
    gradient, hessian, histogram, split_gain = one_round(
        rows, ys, zs, query_tiles, tile_of(doc_scores), tile_of(doc_labels), tile_of(doc_ranks), bin_codes)
    gradient, hessian, histogram, split_gain = publish((gradient, hessian, histogram, split_gain))
    return gradient.reshape(-1), hessian.reshape(-1), histogram, split_gain.reshape(-1)


def solution(mesh):
    return jax.shard_map(
        functools.partial(shards, mesh.shape["row"], 4, mesh.shape["feat"] // 4),
        mesh=mesh,
        in_specs=(P(("row", "feat")), P(("row", "feat")), P(("row", "feat")), P("row", None), P("feat", "row")),
        out_specs=(P(("row", "feat")), P(("row", "feat")), P("feat", None, None), P("feat")),
        check_vma=False,
    )
```

```python
import functools

import jax
import jax.experimental.pallas as pl
import jax.experimental.pallas.tpu as pltpu
import jax.numpy as jnp
from jax import lax
from jax.sharding import PartitionSpec as P

BINS = 256
MAX_TILES = 8
LANES = 128
QUERIES = 64
HIGH, LOW = 8, 32
GROUP = 8
MESH = pl.DeviceIdType.MESH
F32, BF16, F8, I8 = jnp.float32, jnp.bfloat16, jnp.float8_e4m3fn, jnp.int8


def iota(shape, dim):
    return lax.broadcasted_iota(jnp.int32, shape, dim)


def pieces(x):
    first = x.astype(BF16)
    rest = x - first.astype(F32)
    second = rest.astype(BF16)
    third = (rest - second.astype(F32)).astype(BF16)
    return first, second, third


def query_spans(tiles_ref, me):
    first = [jnp.int32(0)] * 8
    count = [jnp.int32(1)] * 8
    start = 8 - me * 8
    for query in range(QUERIES):
        tiles = tiles_ref[0, query]
        for tile in range(8):
            inside = start <= 8 + tile
            first[tile] = jnp.where(inside, start, first[tile])
            count[tile] = jnp.where(inside, tiles, count[tile])
        start = start + tiles
    return first, count


def discount_table():
    place = (iota((8, LANES), 0) * LANES + iota((8, LANES), 1)).astype(F32)
    return place, 1.0 / jnp.log2(place + 2.0)


def span_rows(first, count):
    rows = iota((8, LANES), 0)
    first_rows, count_rows = jnp.zeros((8, LANES), jnp.int32), jnp.zeros((8, LANES), jnp.int32)
    for tile in range(8):
        first_rows = jnp.where(rows == tile, first[tile], first_rows)
        count_rows = jnp.where(rows == tile, count[tile], count_rows)
    return first_rows, count_rows


def query_scale(window, first_rows, count_rows, place, table):
    all_gains = window[1]
    reach = jnp.concatenate([(all_gains >= F32(2 ** level - 1)).astype(F32) for level in range(1, 5)], axis=0)
    reach = jnp.broadcast_to(jnp.sum(reach, axis=1, keepdims=True), (96, LANES))
    above = [jnp.zeros((8, LANES), F32)] * 4
    for tile in range(24):
        member = (first_rows <= tile) & (first_rows + count_rows > tile)
        for level in range(4):
            at = level * 24 + tile
            above[level] = above[level] + jnp.where(member, jnp.broadcast_to(reach[at:at + 1], (8, LANES)), 0.0)
    ideals = []
    for tile in range(8):
        total = jnp.zeros((8, LANES), F32)
        for level in range(4):
            limit = jnp.broadcast_to(above[level][tile:tile + 1], (8, LANES))
            total = total + jnp.where(place < limit, table * F32(2 ** level), 0.0)
        ideals.append(jnp.sum(total, axis=0, keepdims=True))
    ideal = jnp.sum(jnp.concatenate(ideals, axis=0), axis=1, keepdims=True)
    return 1.0 / (1.0 + ideal)


def widen(window, wide, slot):
    for which in range(3):
        turned = jnp.transpose(window[which, slot * 8:slot * 8 + 8, :])
        for tile in range(8):
            wide[which, slot * 8 + tile] = jnp.broadcast_to(turned[:, tile:tile + 1], (LANES, LANES))


def pair_sums(own, wide, first, count):
    odds, gains, discs = own
    grads, hessians = [], []
    rows = 32
    for tile in range(8):
        odds_i, gain_i, disc_i = (jnp.broadcast_to(x[tile:tile + 1], (rows, LANES)) for x in own)

        def column(step, carried):
            at = jnp.where(step < count[tile], jnp.minimum(jnp.maximum(first[tile] + step, 0), 23), 24)
            grad, hess = carried
            for part in range(0, LANES, rows):
                odds_j, gain_j, disc_j = (wide[which, at, part:part + rows, :] for which in range(3))
                inverse = pl.reciprocal(odds_i + odds_j, approx=True)
                delta = gain_i - gain_j
                weight = delta * (jnp.abs(disc_i - disc_j) * inverse)
                grad = grad + weight * jnp.where(delta > 0, odds_j, odds_i)
                hess = hess + jnp.abs(weight) * (inverse * odds_j)
            return grad, hess

        empty = jnp.zeros((rows, LANES), F32)
        grad, hess = lax.fori_loop(0, MAX_TILES, column, (empty, empty), unroll=4)
        grads.append(jnp.sum(grad, axis=0, keepdims=True))
        hessians.append(jnp.sum(hess, axis=0, keepdims=True))
    return jnp.concatenate(grads, axis=0), jnp.concatenate(hessians, axis=0)


def build_matrices(matrices):
    source, target = iota((BINS, BINS), 0), iota((BINS, BINS), 1)
    source_low, source_feat = source >> 3, source & 7
    target_feat, target_low = target >> 5, target & 31
    same = source_feat == target_feat
    for k, flag in enumerate((same & (source_low == target_low), same & (source_low <= target_low), same)):
        matrices[k] = jnp.where(flag, F32(1), F32(0)).astype(BF16)
    pick = ((source & (LOW - 1)) == 0) & ((source >> 5) == (target & 7))
    matrices[3] = jnp.where(pick, F32(1), F32(0)).astype(BF16)


def round_kernel(rows, ys, zs, *refs):
    accumulators = ([pltpu.ACC(k % 2)((2 * HIGH * GROUP, BINS), F32) for k in range(rows)]
                    + [pltpu.ACC(k % 2)((48, BINS), F32) for k in range(3)] + [pltpu.ACC(0)((32, BINS), F32)])
    pl.run_scoped(lambda *accs: round_body(rows, ys, zs, accs[:rows], accs[rows:], *refs), *accumulators)


def round_body(rows, ys, zs, accs, small, tiles_hbm, score_hbm, label_hbm, rank_hbm, codes_hbm,
                 grad_ref, hess_ref, hist_ref, gain_ref,
                 tiles_ref, score_ref, label_ref, rank_ref, codes,
                 window, wide, gathered, spread, matrices, mine, parts, blocks, bests, tops,
                 in_sem, code_sem, halo_send, halo_recv, send_z, recv_z, send_y, recv_y,
                 send_a, recv_a, send_b, recv_b, send_c, recv_c, send_e, recv_e):
    row, feat = lax.axis_index("row"), lax.axis_index("feat")
    feats = ys * zs
    y, z = feat // zs, lax.rem(feat, zs)
    groups = codes.shape[0] // GROUP
    chunks = codes.shape[1] // 1024

    loads = [pltpu.make_async_copy(src, dst, in_sem.at[k]) for k, (src, dst) in enumerate(
        ((score_hbm, score_ref), (label_hbm, label_ref), (rank_hbm, rank_ref), (tiles_hbm, tiles_ref)))]
    for load in loads:
        load.start()
    y_low, y_high = lax.rem(y, 2), y // 2

    def y_block(step):
        return lax.rem(y_high + step // 2, 2) * 2 + lax.rem(y_low + step % 2, 2)

    def code_load(step):
        docs = pl.ds(pl.multiple_of(y_block(step) * (zs * 1024), zs * 1024), zs * 1024)
        return pltpu.make_async_copy(codes_hbm.at[:, docs], codes.at[:, docs], code_sem.at[step])


    barrier = pltpu.get_barrier_semaphore()

    def at_row(step):
        return {"row": lax.rem(row + step, rows)}

    def at_z(step):
        return {"feat": y * zs + lax.rem(z + step, zs)}

    def at_y(step):
        return {"feat": y_block(step) * zs + z}

    def at_row_y(step):
        return {"row": lax.rem(row + step // 2, rows), "feat": y_block(step % 2) * zs + z}

    def at_z_y(step):
        return {"feat": y_block(step % 2 * 2) * zs + lax.rem(z + step // 2, zs)}

    def at_feat(step):
        return {"feat": lax.rem(feat + step, feats)}

    def signal(device):
        pl.semaphore_signal(barrier, inc=1, device_id=device, device_id_type=MESH)

    signal(at_feat(1))
    signal(at_feat(feats - 1))
    for step in range(1, 2 * zs):
        signal(at_z_y(step))
    signal(at_y(3))
    for step in range(1, 2 * rows):
        signal(at_row_y(step))
    for load in loads:
        load.wait()

    odds = jnp.exp(score_ref[...])
    gains = (jnp.left_shift(1, label_ref[...]) - 1).astype(F32)
    discs = 1.0 / jnp.log2(rank_ref[...].astype(F32) + 2.0)
    own = (odds, gains, discs)
    for which in range(3):
        window[which, 8:16, :] = own[which]
    pl.semaphore_wait(barrier, 2 + 2 * zs - 1 + 1 + 2 * rows - 1)
    halos = []
    for side, (target, place) in enumerate(((feats - 1, 16), (1, 0))):
        copy = pltpu.make_async_remote_copy(
            src_ref=window.at[:, pl.ds(8, 8), :], dst_ref=window.at[:, pl.ds(place, 8), :],
            send_sem=halo_send.at[side], recv_sem=halo_recv.at[side],
            device_id=at_feat(target), device_id_type=MESH)
        copy.start()
        halos.append(copy)
    code_load(0).start()
    for which, value in enumerate((0.0, -1.0, 0.0)):
        wide[which, 24] = jnp.full((LANES, LANES), value, F32)
    build_matrices(matrices)
    first, count = query_spans(tiles_ref, feat)
    span = span_rows(first, count)
    place, table = discount_table()
    widen(window, wide, 1)
    for copy in halos:
        copy.wait()
    for step in range(1, ys):
        code_load(step).start()
    widen(window, wide, 0)
    widen(window, wide, 2)
    scale = query_scale(window, *span, place, table)
    grad, hess = pair_sums(own, wide, first, count)
    grad = -grad * scale
    hess = hess * (odds * scale)
    grad_ref[...] = grad
    hess_ref[...] = hess
    gathered[feat] = jnp.concatenate([grad, hess], axis=0).astype(BF16)

    def over_z(step):
        return pltpu.make_async_remote_copy(
            src_ref=gathered.at[feat], dst_ref=gathered.at[feat], send_sem=send_z.at[step], recv_sem=recv_z.at[step],
            device_id=at_z(step), device_id_type=MESH)

    def over_y(step):
        block = gathered.at[pl.ds(y * zs, zs)]
        return pltpu.make_async_remote_copy(
            src_ref=block, dst_ref=block, send_sem=send_y.at[step], recv_sem=recv_y.at[step],
            device_id=at_y(step), device_id_type=MESH)

    offsets = [(turn + 1) // 2 if turn % 2 else zs - turn // 2 for turn in range(1, zs)]
    for step in offsets:
        over_z(step).start()
    code_load(0).wait()

    def scatter(group):
        return pltpu.make_async_remote_copy(
            src_ref=mine.at[group], dst_ref=parts.at[row], send_sem=send_a.at[group], recv_sem=recv_a.at[row],
            device_id={"row": jnp.int32(group)}, device_id_type=MESH)

    def arrival(step):
        source = lax.rem(row + step, rows)
        return pltpu.make_async_remote_copy(
            src_ref=parts.at[source], dst_ref=parts.at[source], send_sem=send_a.at[source], recv_sem=recv_a.at[source],
            device_id=at_row(step), device_id_type=MESH)

    zero = jnp.zeros((), BF16)

    def arrived(offset):
        over_z(zs - offset).wait_recv()

    def owner_of(turn):
        inner = lax.rem(turn, zs)
        odd = lax.rem(inner, 2)
        offset = odd * ((inner + 1) // 2) + (1 - odd) * (zs - inner // 2)
        outer = turn // zs
        owner_y = lax.rem(y_high + outer // 2, 2) * 2 + lax.rem(y_low + lax.rem(outer, 2), 2)
        return owner_y * zs + lax.rem(z + offset, zs)

    def add_chunks(owners):
        for slot, owner in enumerate(owners):
            part = gathered[owner].astype(F32)
            for which in range(2):
                for tile in range(8):
                    line = which * 8 + tile
                    at = slot * 1024 + tile * LANES
                    spread[which, :, at:at + LANES] = jnp.broadcast_to(part[line:line + 1], (16, LANES)).astype(BF16)
        for slot, owner in enumerate(owners):
            for k in range(1024 // BINS):
                at = pl.ds(pl.multiple_of(owner * 1024 + k * BINS, BINS), BINS)
                there = slot * 1024 + k * BINS
                lam = [spread[which, :, there:there + BINS] for which in range(2)]
                for group in range(groups):
                    code = codes[group * GROUP:(group + 1) * GROUP, at]
                    high = (code >> 5).astype(F32)
                    high = jnp.concatenate([high, high - 1.0], axis=0).astype(BF16)
                    hits = [high == jnp.array(2 * k, BF16) for k in range(HIGH // 2)]
                    lhs = jnp.concatenate([jnp.where(hit, value, zero) for value in lam for hit in hits], axis=0)
                    low = code & (LOW - 1)
                    low = jnp.concatenate([low - k for k in range(4)], axis=0).astype(I8)
                    rhs = jnp.concatenate(
                        [jnp.where(low == jnp.array(4 * k, I8), jnp.ones((), F8), jnp.zeros((), F8))
                         for k in range(LOW // 4)], axis=0)
                    stage = group // 2 % 2
                    pltpu.matmul_push_rhs(rhs, stage, group % 2, transpose=True)
                    pltpu.matmul_acc_lhs(accs[group], lhs, load_staged_rhs=stage)

    @pl.loop(0, 2)
    def _(turn):
        @pl.when(turn == 1)
        def _():
            arrived(offsets[0])

        add_chunks([owner_of(turn)])

    for offset in offsets[1:3]:
        arrived(offset)
    add_chunks([owner_of(jnp.int32(turn)) for turn in (2, 3)])
    for offset in offsets[3:]:
        arrived(offset)
    for step in range(1, ys):
        over_y(step).start()

    @pl.loop(1, chunks // 4)
    def _(four):
        turn = 4 * four
        for step in range(1, ys):
            @pl.when(turn == step * zs)
            def _():
                over_y(step).wait_recv()
                code_load(step).wait()

        add_chunks([owner_of(turn + k) for k in range(4)])

    shape = (2 * HIGH, GROUP, BINS)
    same = iota(shape, 1) == (iota(shape, 2) & (GROUP - 1))
    for group in range(groups):
        total = pltpu.matmul_pop(accs[group]).reshape(shape)
        mine[group] = jnp.sum(jnp.where(same, total, 0.0), axis=1)

        @pl.when(row != group)
        def _():
            scatter(group).start()


    for step in range(1, zs):
        over_z(step).wait_send()
    for step in range(1, ys):
        over_y(step).wait_send()
    parts[row] = mine[row]
    for step in range(1, rows):
        arrival(step).wait_recv()
    summed = parts[0]
    for k in range(1, rows):
        summed = summed + parts[k]

    split = jnp.concatenate(pieces(summed), axis=0)
    for k in range(3):
        pltpu.matmul_push_rhs(matrices[k], k // 2, k % 2)
        pltpu.matmul_acc_lhs(small[k], split, load_staged_rhs=k // 2)

    def product(k):
        full = pltpu.matmul_pop(small[k])
        return full[0:16] + (full[16:32] + full[32:48])

    left, across, moved = product(1), product(2), product(0)
    running = [jnp.zeros((1, BINS), F32)] * 2
    sides = [[], []]
    for which in range(2):
        for k in range(HIGH):
            at = which * HIGH + k
            sides[which].append(left[at:at + 1] + running[which])
            running[which] = running[which] + across[at:at + 1]
    grad_left, hess_left = (jnp.concatenate(side, axis=0) for side in sides)
    grad_all, hess_all = running
    grad_right = grad_all - grad_left
    gain = (grad_left * grad_left / (hess_left + 1.0)
            + grad_right * grad_right / (hess_all - hess_left + 1.0)
            - grad_all * grad_all / (hess_all + 1.0))
    shape = (HIGH, BINS)
    last = (iota(shape, 0) == HIGH - 1) & ((iota(shape, 1) & (LOW - 1)) == LOW - 1)
    gain = jnp.where(last, -jnp.inf, gain)
    place_a = row * 2 + y_low
    bests[place_a] = jnp.max(gain, axis=0, keepdims=True)

    def send_best(step):
        return pltpu.make_async_remote_copy(
            src_ref=bests.at[place_a], dst_ref=bests.at[place_a], send_sem=send_b.at[step], recv_sem=recv_b.at[step],
            device_id=at_row_y(step), device_id_type=MESH)

    for step in range(1, 2 * rows):
        send_best(step).start()

    def send_block(step):
        return pltpu.make_async_remote_copy(
            src_ref=blocks.at[row], dst_ref=blocks.at[row], send_sem=send_e.at[step], recv_sem=recv_e.at[step],
            device_id=at_row(step), device_id_type=MESH)

    block = (iota(shape, 1) >> 5) == iota(shape, 0)
    for which in range(2):
        whole_rows = moved[which * HIGH:(which + 1) * HIGH]
        placed = jnp.zeros(shape, F32)
        for shift in range(GROUP):
            turned = whole_rows if shift == 0 else pltpu.roll(whole_rows, shift * LOW, 1)
            turned = jnp.where(block, turned, 0.0)
            placed = placed + (turned if shift == 0 else pltpu.roll(turned, GROUP - shift, 0))
        blocks[row, :, which, :] = placed

    for step in range(1, 2 * rows):
        send_best(step).wait()
    top = jnp.max(bests[...], axis=0)
    place_b = z * 2 + y_high
    tops[place_b] = jnp.broadcast_to(jnp.max(top, axis=1, keepdims=True), (1, LANES))

    def send_top(step):
        return pltpu.make_async_remote_copy(
            src_ref=tops.at[place_b], dst_ref=tops.at[place_b], send_sem=send_c.at[step], recv_sem=recv_c.at[step],
            device_id=at_z_y(step), device_id_type=MESH)

    for step in range(1, 2 * zs):
        send_top(step).start()
    for step in range(1, rows):
        send_block(step).start()
    every = jnp.concatenate([bests[k * 2 + y_low] for k in range(rows)], axis=0)
    for shift in (1, 2, 4, 8, 16):
        every = jnp.maximum(every, pltpu.roll(every, BINS - shift, 1))
    every = jnp.where((iota((rows, BINS), 1) & (LOW - 1)) == 0, every, 0.0)
    split = jnp.concatenate([piece.astype(F32) for piece in pieces(every)] + [jnp.zeros((rows, BINS), F32)], axis=0)
    pltpu.matmul_push_rhs(matrices[3], 0, 0)
    pltpu.matmul_acc_lhs(small[3], split.astype(BF16), load_staged_rhs=0)
    full = pltpu.matmul_pop(small[3])
    chosen = full[0:rows] + (full[rows:2 * rows] + full[2 * rows:3 * rows])
    owned = (iota((rows, BINS), 1) >> 3) == iota((rows, BINS), 0)
    line = jnp.sum(jnp.where(owned, chosen, 0.0), axis=0, keepdims=True)
    for step in range(1, rows):
        send_block(step).wait()
    for k in range(rows):
        hist_ref[k * GROUP:(k + 1) * GROUP] = blocks[k]
    for group in range(groups):
        @pl.when(row != group)
        def _():
            scatter(group).wait_send()
    for step in range(1, 2 * zs):
        send_top(step).wait()
    largest = jnp.max(tops[...], axis=0)
    gain_ref[...] = (line[:, :LANES] / (largest + 1e-6))[:, :rows * GROUP]


def one_round(rows, ys, zs, tiles, scores, labels, ranks, codes):
    vmem = pl.BlockSpec(memory_space=pltpu.VMEM)
    hbm = pl.BlockSpec(memory_space=pltpu.HBM)
    here, docs = codes.shape
    groups = here // GROUP
    feats = ys * zs
    block = pltpu.VMEM((8, LANES), F32)
    dma = pltpu.SemaphoreType.DMA
    pair = lambda n: [dma((n,)), dma((n,))]
    return pl.pallas_call(
        functools.partial(round_kernel, rows, ys, zs),
        out_shape=(block, block, pltpu.VMEM((here, 2, BINS), F32), pltpu.VMEM((1, here), F32)),
        in_specs=[hbm] * 5,
        out_specs=(vmem,) * 4,
        scratch_shapes=[
            pltpu.SMEM((1, QUERIES), jnp.int32), pltpu.VMEM((8, LANES), F32), pltpu.VMEM((8, LANES), jnp.int32),
            pltpu.VMEM((8, LANES), jnp.int32), pltpu.VMEM((here, docs), jnp.int32),
            pltpu.VMEM((3, 24, LANES), F32), pltpu.VMEM((3, 25, LANES, LANES), F32), pltpu.VMEM((feats, 16, LANES), BF16),
            pltpu.VMEM((2, 16, 4096), BF16), pltpu.VMEM((4, BINS, BINS), BF16),
            pltpu.VMEM((groups, 2 * HIGH, BINS), F32), pltpu.VMEM((rows, 2 * HIGH, BINS), F32),
            pltpu.VMEM((rows, GROUP, 2, BINS), F32), pltpu.VMEM((2 * rows, 1, BINS), F32),
            pltpu.VMEM((2 * zs, 1, LANES), F32),
            dma((4,)), dma((ys,)), *pair(2), *pair(zs), *pair(ys),
            *pair(rows), *pair(2 * rows), *pair(2 * zs), *pair(rows),
        ],
        compiler_params=pltpu.CompilerParams(collective_id=0, has_side_effects=True, vmem_limit_bytes=60 * 2 ** 20),
        name="round",
    )(tiles, scores, labels, ranks, codes)


def publish_kernel(*refs):
    sems = refs[-1]
    half = (len(refs) - 1) // 2
    copies = [pltpu.make_async_copy(refs[k], refs[half + k], sems.at[k]) for k in range(half)]
    for copy in copies:
        copy.start()
    for copy in copies:
        copy.wait()


def publish(arrays):
    hbm = pl.BlockSpec(memory_space=pltpu.HBM)
    return pl.pallas_call(
        publish_kernel,
        out_shape=tuple(jax.ShapeDtypeStruct(x.shape, x.dtype) for x in arrays),
        in_specs=[pl.BlockSpec(memory_space=pltpu.VMEM)] * len(arrays),
        out_specs=(hbm,) * len(arrays),
        scratch_shapes=[pltpu.SemaphoreType.DMA((len(arrays),))],
        name="publish",
    )(*[pltpu.with_memory_space_constraint(x, pltpu.VMEM) for x in arrays])


def shards(rows, ys, zs, doc_scores, doc_labels, doc_ranks, query_tiles, bin_codes):
    tile_of = lambda x: x.reshape(8, LANES)
    gradient, hessian, histogram, split_gain = one_round(
        rows, ys, zs, query_tiles, tile_of(doc_scores), tile_of(doc_labels), tile_of(doc_ranks), bin_codes)
    gradient, hessian, histogram, split_gain = publish((gradient, hessian, histogram, split_gain))
    return gradient.reshape(-1), hessian.reshape(-1), histogram, split_gain.reshape(-1)


def solution(mesh):
    return jax.shard_map(
        functools.partial(shards, mesh.shape["row"], 4, mesh.shape["feat"] // 4),
        mesh=mesh,
        in_specs=(P(("row", "feat")), P(("row", "feat")), P(("row", "feat")), P("row", None), P("feat", "row")),
        out_specs=(P(("row", "feat")), P(("row", "feat")), P("feat", None, None), P("feat")),
        check_vma=False,
    )
```

```python
import functools

import jax
import jax.experimental.pallas as pl
import jax.experimental.pallas.tpu as pltpu
import jax.numpy as jnp
from jax import lax
from jax.sharding import PartitionSpec as P

BINS = 256
MAX_TILES = 8
LANES = 128
QUERIES = 64
HIGH, LOW = 8, 32
GROUP = 8
MESH = pl.DeviceIdType.MESH
F32, BF16, F8, I8 = jnp.float32, jnp.bfloat16, jnp.float8_e4m3fn, jnp.int8


def iota(shape, dim):
    return lax.broadcasted_iota(jnp.int32, shape, dim)


def pieces(x):
    first = x.astype(BF16)
    rest = x - first.astype(F32)
    second = rest.astype(BF16)
    third = (rest - second.astype(F32)).astype(BF16)
    return first, second, third


def query_spans(tiles_ref, me):
    first = [jnp.int32(0)] * 8
    count = [jnp.int32(1)] * 8
    start = 8 - me * 8
    for query in range(QUERIES):
        tiles = tiles_ref[0, query]
        for tile in range(8):
            inside = start <= 8 + tile
            first[tile] = jnp.where(inside, start, first[tile])
            count[tile] = jnp.where(inside, tiles, count[tile])
        start = start + tiles
    return first, count


def discount_table():
    place = (iota((8, LANES), 0) * LANES + iota((8, LANES), 1)).astype(F32)
    return place, 1.0 / jnp.log2(place + 2.0)


def span_rows(first, count):
    rows = iota((8, LANES), 0)
    first_rows, count_rows = jnp.zeros((8, LANES), jnp.int32), jnp.zeros((8, LANES), jnp.int32)
    for tile in range(8):
        first_rows = jnp.where(rows == tile, first[tile], first_rows)
        count_rows = jnp.where(rows == tile, count[tile], count_rows)
    return first_rows, count_rows


def query_scale(window, first_rows, count_rows, place, table):
    all_gains = window[1]
    reach = jnp.concatenate([(all_gains >= F32(2 ** level - 1)).astype(F32) for level in range(1, 5)], axis=0)
    reach = jnp.broadcast_to(jnp.sum(reach, axis=1, keepdims=True), (96, LANES))
    above = [jnp.zeros((8, LANES), F32)] * 4
    for tile in range(24):
        member = (first_rows <= tile) & (first_rows + count_rows > tile)
        for level in range(4):
            at = level * 24 + tile
            above[level] = above[level] + jnp.where(member, jnp.broadcast_to(reach[at:at + 1], (8, LANES)), 0.0)
    ideals = []
    for tile in range(8):
        total = jnp.zeros((8, LANES), F32)
        for level in range(4):
            limit = jnp.broadcast_to(above[level][tile:tile + 1], (8, LANES))
            total = total + jnp.where(place < limit, table * F32(2 ** level), 0.0)
        ideals.append(jnp.sum(total, axis=0, keepdims=True))
    ideal = jnp.sum(jnp.concatenate(ideals, axis=0), axis=1, keepdims=True)
    return 1.0 / (1.0 + ideal)


def widen(window, wide, slot):
    for which in range(3):
        turned = jnp.transpose(window[which, slot * 8:slot * 8 + 8, :])
        for tile in range(8):
            wide[which, slot * 8 + tile] = jnp.broadcast_to(turned[:, tile:tile + 1], (LANES, LANES))


def pair_sums(own, wide, first, count):
    odds, gains, discs = own
    grads, hessians = [], []
    rows = 32
    for tile in range(8):
        odds_i, gain_i, disc_i = (jnp.broadcast_to(x[tile:tile + 1], (rows, LANES)) for x in own)

        def column(step, carried):
            at = jnp.where(step < count[tile], jnp.minimum(jnp.maximum(first[tile] + step, 0), 23), 24)
            grad, hess = carried
            for part in range(0, LANES, rows):
                odds_j, gain_j, disc_j = (wide[which, at, part:part + rows, :] for which in range(3))
                inverse = pl.reciprocal(odds_i + odds_j, approx=True)
                delta = gain_i - gain_j
                weight = delta * (jnp.abs(disc_i - disc_j) * inverse)
                grad = grad + weight * jnp.where(delta > 0, odds_j, odds_i)
                hess = hess + jnp.abs(weight) * (inverse * odds_j)
            return grad, hess

        empty = jnp.zeros((rows, LANES), F32)
        grad, hess = lax.fori_loop(0, MAX_TILES, column, (empty, empty), unroll=8)
        grads.append(jnp.sum(grad, axis=0, keepdims=True))
        hessians.append(jnp.sum(hess, axis=0, keepdims=True))
    return jnp.concatenate(grads, axis=0), jnp.concatenate(hessians, axis=0)


def build_matrices(matrices):
    source, target = iota((BINS, BINS), 0), iota((BINS, BINS), 1)
    source_low, source_feat = source >> 3, source & 7
    target_feat, target_low = target >> 5, target & 31
    same = source_feat == target_feat
    for k, flag in enumerate((same & (source_low == target_low), same & (source_low <= target_low), same)):
        matrices[k] = jnp.where(flag, F32(1), F32(0)).astype(BF16)
    pick = ((source & (LOW - 1)) == 0) & ((source >> 5) == (target & 7))
    matrices[3] = jnp.where(pick, F32(1), F32(0)).astype(BF16)


def round_kernel(rows, ys, zs, *refs):
    accumulators = ([pltpu.ACC(k % 2)((2 * HIGH * GROUP, BINS), F32) for k in range(rows)]
                    + [pltpu.ACC(mxu)((48, BINS), F32) for mxu in (0, 0, 1)] + [pltpu.ACC(1)((32, BINS), F32)])
    pl.run_scoped(lambda *accs: round_body(rows, ys, zs, accs[:rows], accs[rows:], *refs), *accumulators)


def round_body(rows, ys, zs, accs, small, tiles_hbm, score_hbm, label_hbm, rank_hbm, codes_hbm,
                 grad_ref, hess_ref, hist_ref, gain_ref,
                 tiles_ref, score_ref, label_ref, rank_ref, codes,
                 window, wide, gathered, spread, matrices, mine, parts, blocks, bests, tops,
                 in_sem, code_sem, halo_send, halo_recv, send_z, recv_z, send_y, recv_y,
                 send_a, recv_a, send_b, recv_b, send_c, recv_c, send_e, recv_e):
    row, feat = lax.axis_index("row"), lax.axis_index("feat")
    feats = ys * zs
    y, z = feat // zs, lax.rem(feat, zs)
    groups = codes.shape[0] // GROUP
    chunks = codes.shape[1] // 1024

    loads = [pltpu.make_async_copy(src, dst, in_sem.at[k]) for k, (src, dst) in enumerate(
        ((score_hbm, score_ref), (label_hbm, label_ref), (rank_hbm, rank_ref), (tiles_hbm, tiles_ref)))]
    for load in loads:
        load.start()
    y_low, y_high = lax.rem(y, 2), y // 2

    def y_block(step):
        return lax.rem(y_high + step // 2, 2) * 2 + lax.rem(y_low + step % 2, 2)

    def code_load(step):
        docs = pl.ds(pl.multiple_of(y_block(step) * (zs * 1024), zs * 1024), zs * 1024)
        return pltpu.make_async_copy(codes_hbm.at[:, docs], codes.at[:, docs], code_sem.at[step])


    barrier = pltpu.get_barrier_semaphore()

    def at_row(step):
        return {"row": lax.rem(row + step, rows)}

    def at_z(step):
        return {"feat": y * zs + lax.rem(z + step, zs)}

    def at_y(step):
        return {"feat": y_block(step) * zs + z}

    def at_row_y(step):
        return {"row": lax.rem(row + step // 2, rows), "feat": y_block(step % 2) * zs + z}

    def at_z_y(step):
        return {"feat": y_block(step % 2 * 2) * zs + lax.rem(z + step // 2, zs)}

    def at_feat(step):
        return {"feat": lax.rem(feat + step, feats)}

    def signal(device):
        pl.semaphore_signal(barrier, inc=1, device_id=device, device_id_type=MESH)

    signal(at_feat(1))
    signal(at_feat(feats - 1))
    for step in range(1, 2 * zs):
        signal(at_z_y(step))
    signal(at_y(3))
    for step in range(1, 2 * rows):
        signal(at_row_y(step))
    for load in loads:
        load.wait()

    odds = jnp.exp(score_ref[...])
    gains = (jnp.left_shift(1, label_ref[...]) - 1).astype(F32)
    discs = 1.0 / jnp.log2(rank_ref[...].astype(F32) + 2.0)
    own = (odds, gains, discs)
    for which in range(3):
        window[which, 8:16, :] = own[which]
    pl.semaphore_wait(barrier, 2 + 2 * zs - 1 + 1 + 2 * rows - 1)
    halos = []
    for side, (target, place) in enumerate(((feats - 1, 16), (1, 0))):
        copy = pltpu.make_async_remote_copy(
            src_ref=window.at[:, pl.ds(8, 8), :], dst_ref=window.at[:, pl.ds(place, 8), :],
            send_sem=halo_send.at[side], recv_sem=halo_recv.at[side],
            device_id=at_feat(target), device_id_type=MESH)
        copy.start()
        halos.append(copy)
    code_load(0).start()
    for which, value in enumerate((0.0, -1.0, 0.0)):
        wide[which, 24] = jnp.full((LANES, LANES), value, F32)
    build_matrices(matrices)
    first, count = query_spans(tiles_ref, feat)
    span = span_rows(first, count)
    place, table = discount_table()
    widen(window, wide, 1)
    for copy in halos:
        copy.wait()
    for step in range(1, ys):
        code_load(step).start()
    widen(window, wide, 0)
    widen(window, wide, 2)
    scale = query_scale(window, *span, place, table)
    grad, hess = pair_sums(own, wide, first, count)
    grad = -grad * scale
    hess = hess * (odds * scale)
    grad_ref[...] = grad
    hess_ref[...] = hess
    gathered[feat] = jnp.concatenate([grad, hess], axis=0).astype(BF16)

    def over_z(step):
        return pltpu.make_async_remote_copy(
            src_ref=gathered.at[feat], dst_ref=gathered.at[feat], send_sem=send_z.at[step], recv_sem=recv_z.at[step],
            device_id=at_z(step), device_id_type=MESH)

    def over_y(step):
        block = gathered.at[pl.ds(y * zs, zs)]
        return pltpu.make_async_remote_copy(
            src_ref=block, dst_ref=block, send_sem=send_y.at[step], recv_sem=recv_y.at[step],
            device_id=at_y(step), device_id_type=MESH)

    offsets = [(turn + 1) // 2 if turn % 2 else zs - turn // 2 for turn in range(1, zs)]
    for step in offsets:
        over_z(step).start()
    code_load(0).wait()

    def scatter(group):
        return pltpu.make_async_remote_copy(
            src_ref=mine.at[group], dst_ref=parts.at[row], send_sem=send_a.at[group], recv_sem=recv_a.at[row],
            device_id={"row": jnp.int32(group)}, device_id_type=MESH)

    def arrival(step):
        source = lax.rem(row + step, rows)
        return pltpu.make_async_remote_copy(
            src_ref=parts.at[source], dst_ref=parts.at[source], send_sem=send_a.at[source], recv_sem=recv_a.at[source],
            device_id=at_row(step), device_id_type=MESH)

    zero = jnp.zeros((), BF16)

    def arrived(offset):
        over_z(zs - offset).wait_recv()

    def owner_of(turn):
        inner = lax.rem(turn, zs)
        odd = lax.rem(inner, 2)
        offset = odd * ((inner + 1) // 2) + (1 - odd) * (zs - inner // 2)
        outer = turn // zs
        owner_y = lax.rem(y_high + outer // 2, 2) * 2 + lax.rem(y_low + lax.rem(outer, 2), 2)
        return owner_y * zs + lax.rem(z + offset, zs)

    def add_chunks(owners):
        for slot, owner in enumerate(owners):
            part = gathered[owner].astype(F32)
            for which in range(2):
                for tile in range(8):
                    line = which * 8 + tile
                    at = slot * 1024 + tile * LANES
                    spread[which, :, at:at + LANES] = jnp.broadcast_to(part[line:line + 1], (16, LANES)).astype(BF16)
        for slot, owner in enumerate(owners):
            for k in range(1024 // BINS):
                at = pl.ds(pl.multiple_of(owner * 1024 + k * BINS, BINS), BINS)
                there = slot * 1024 + k * BINS
                lam = [spread[which, :, there:there + BINS] for which in range(2)]
                for group in range(groups):
                    code = codes[group * GROUP:(group + 1) * GROUP, at]
                    high = (code >> 5).astype(F32)
                    high = jnp.concatenate([high, high - 1.0], axis=0).astype(BF16)
                    hits = [high == jnp.array(2 * k, BF16) for k in range(HIGH // 2)]
                    lhs = jnp.concatenate([jnp.where(hit, value, zero) for value in lam for hit in hits], axis=0)
                    low = code & (LOW - 1)
                    low = jnp.concatenate([low - k for k in range(4)], axis=0).astype(I8)
                    rhs = jnp.concatenate(
                        [jnp.where(low == jnp.array(4 * k, I8), jnp.ones((), F8), jnp.zeros((), F8))
                         for k in range(LOW // 4)], axis=0)
                    stage = group // 2 % 2
                    pltpu.matmul_push_rhs(rhs, stage, group % 2, transpose=True)
                    pltpu.matmul_acc_lhs(accs[group], lhs, load_staged_rhs=stage)

    @pl.loop(0, 2)
    def _(turn):
        @pl.when(turn == 1)
        def _():
            arrived(offsets[0])

        add_chunks([owner_of(turn)])

    for offset in offsets[1:3]:
        arrived(offset)
    add_chunks([owner_of(jnp.int32(turn)) for turn in (2, 3)])
    for offset in offsets[3:]:
        arrived(offset)
    for step in range(1, ys):
        over_y(step).start()

    @pl.loop(1, chunks // 4)
    def _(four):
        turn = 4 * four
        for step in range(1, ys):
            @pl.when(turn == step * zs)
            def _():
                over_y(step).wait_recv()
                code_load(step).wait()

        add_chunks([owner_of(turn + k) for k in range(4)])

    shape = (2 * HIGH, GROUP, BINS)
    same = iota(shape, 1) == (iota(shape, 2) & (GROUP - 1))
    for batch in range(0, groups, 4):
        for group in range(batch, batch + 4):
            total = pltpu.matmul_pop(accs[group]).reshape(shape)
            mine[group] = jnp.sum(jnp.where(same, total, 0.0), axis=1)
        for group in range(batch, batch + 4):
            @pl.when(row != group)
            def _():
                scatter(group).start()

    for k, mxu, stage in ((1, 0, 0), (2, 1, 0), (0, 0, 1), (3, 1, 1)):
        pltpu.matmul_push_rhs(matrices[k], stage, mxu)
    for step in range(1, zs):
        over_z(step).wait_send()
    for step in range(1, ys):
        over_y(step).wait_send()
    parts[row] = mine[row]
    for step in range(1, rows):
        arrival(step).wait_recv()
    summed = parts[0]
    for k in range(1, rows):
        summed = summed + parts[k]

    split = jnp.concatenate(pieces(summed), axis=0)
    for k, stage in ((1, 0), (2, 0), (0, 1)):
        pltpu.matmul_acc_lhs(small[k], split, load_staged_rhs=stage)

    def product(k):
        full = pltpu.matmul_pop(small[k])
        return full[0:16] + (full[16:32] + full[32:48])

    left, across, moved = product(1), product(2), product(0)
    running = [jnp.zeros((1, BINS), F32)] * 2
    sides = [[], []]
    for which in range(2):
        for k in range(HIGH):
            at = which * HIGH + k
            sides[which].append(left[at:at + 1] + running[which])
            running[which] = running[which] + across[at:at + 1]
    grad_left, hess_left = (jnp.concatenate(side, axis=0) for side in sides)
    grad_all, hess_all = running
    grad_right = grad_all - grad_left
    gain = (grad_left * grad_left / (hess_left + 1.0)
            + grad_right * grad_right / (hess_all - hess_left + 1.0)
            - grad_all * grad_all / (hess_all + 1.0))
    shape = (HIGH, BINS)
    last = (iota(shape, 0) == HIGH - 1) & ((iota(shape, 1) & (LOW - 1)) == LOW - 1)
    gain = jnp.where(last, -jnp.inf, gain)
    place_a = row * 2 + y_low
    bests[place_a] = jnp.max(gain, axis=0, keepdims=True)

    def send_best(step):
        return pltpu.make_async_remote_copy(
            src_ref=bests.at[place_a], dst_ref=bests.at[place_a], send_sem=send_b.at[step], recv_sem=recv_b.at[step],
            device_id=at_row_y(step), device_id_type=MESH)

    for step in range(1, 2 * rows):
        send_best(step).start()

    def send_block(step):
        return pltpu.make_async_remote_copy(
            src_ref=blocks.at[row], dst_ref=blocks.at[row], send_sem=send_e.at[step], recv_sem=recv_e.at[step],
            device_id=at_row(step), device_id_type=MESH)

    block = (iota(shape, 1) >> 5) == iota(shape, 0)
    for which in range(2):
        whole_rows = moved[which * HIGH:(which + 1) * HIGH]
        placed = jnp.zeros(shape, F32)
        for shift in range(GROUP):
            turned = whole_rows if shift == 0 else pltpu.roll(whole_rows, shift * LOW, 1)
            turned = jnp.where(block, turned, 0.0)
            placed = placed + (turned if shift == 0 else pltpu.roll(turned, GROUP - shift, 0))
        blocks[row, :, which, :] = placed

    for step in range(1, 2 * rows):
        send_best(step).wait()
    top = jnp.max(bests[...], axis=0)
    place_b = z * 2 + y_high
    tops[place_b] = jnp.broadcast_to(jnp.max(top, axis=1, keepdims=True), (1, LANES))

    def send_top(step):
        return pltpu.make_async_remote_copy(
            src_ref=tops.at[place_b], dst_ref=tops.at[place_b], send_sem=send_c.at[step], recv_sem=recv_c.at[step],
            device_id=at_z_y(step), device_id_type=MESH)

    for step in range(1, 2 * zs):
        send_top(step).start()
    for step in range(1, rows):
        send_block(step).start()
    every = jnp.concatenate([bests[k * 2 + y_low] for k in range(rows)], axis=0)
    for shift in (1, 2, 4, 8, 16):
        every = jnp.maximum(every, pltpu.roll(every, BINS - shift, 1))
    every = jnp.where((iota((rows, BINS), 1) & (LOW - 1)) == 0, every, 0.0)
    split = jnp.concatenate([piece.astype(F32) for piece in pieces(every)] + [jnp.zeros((rows, BINS), F32)], axis=0)
    pltpu.matmul_acc_lhs(small[3], split.astype(BF16), load_staged_rhs=1)
    full = pltpu.matmul_pop(small[3])
    chosen = full[0:rows] + (full[rows:2 * rows] + full[2 * rows:3 * rows])
    owned = (iota((rows, BINS), 1) >> 3) == iota((rows, BINS), 0)
    line = jnp.sum(jnp.where(owned, chosen, 0.0), axis=0, keepdims=True)
    for step in range(1, rows):
        send_block(step).wait()
    for k in range(rows):
        hist_ref[k * GROUP:(k + 1) * GROUP] = blocks[k]
    for group in range(groups):
        @pl.when(row != group)
        def _():
            scatter(group).wait_send()
    for step in range(1, 2 * zs):
        send_top(step).wait()
    largest = jnp.max(tops[...], axis=0)
    gain_ref[...] = (line[:, :LANES] / (largest + 1e-6))[:, :rows * GROUP]


def one_round(rows, ys, zs, tiles, scores, labels, ranks, codes):
    vmem = pl.BlockSpec(memory_space=pltpu.VMEM)
    hbm = pl.BlockSpec(memory_space=pltpu.HBM)
    here, docs = codes.shape
    groups = here // GROUP
    feats = ys * zs
    block = pltpu.VMEM((8, LANES), F32)
    dma = pltpu.SemaphoreType.DMA
    pair = lambda n: [dma((n,)), dma((n,))]
    return pl.pallas_call(
        functools.partial(round_kernel, rows, ys, zs),
        out_shape=(block, block, pltpu.VMEM((here, 2, BINS), F32), pltpu.VMEM((1, here), F32)),
        in_specs=[hbm] * 5,
        out_specs=(vmem,) * 4,
        scratch_shapes=[
            pltpu.SMEM((1, QUERIES), jnp.int32), pltpu.VMEM((8, LANES), F32), pltpu.VMEM((8, LANES), jnp.int32),
            pltpu.VMEM((8, LANES), jnp.int32), pltpu.VMEM((here, docs), jnp.int32),
            pltpu.VMEM((3, 24, LANES), F32), pltpu.VMEM((3, 25, LANES, LANES), F32), pltpu.VMEM((feats, 16, LANES), BF16),
            pltpu.VMEM((2, 16, 4096), BF16), pltpu.VMEM((4, BINS, BINS), BF16),
            pltpu.VMEM((groups, 2 * HIGH, BINS), F32), pltpu.VMEM((rows, 2 * HIGH, BINS), F32),
            pltpu.VMEM((rows, GROUP, 2, BINS), F32), pltpu.VMEM((2 * rows, 1, BINS), F32),
            pltpu.VMEM((2 * zs, 1, LANES), F32),
            dma((4,)), dma((ys,)), *pair(2), *pair(zs), *pair(ys),
            *pair(rows), *pair(2 * rows), *pair(2 * zs), *pair(rows),
        ],
        compiler_params=pltpu.CompilerParams(collective_id=0, has_side_effects=True, vmem_limit_bytes=60 * 2 ** 20),
        name="round",
    )(tiles, scores, labels, ranks, codes)


def publish_kernel(*refs):
    sems = refs[-1]
    half = (len(refs) - 1) // 2
    copies = [pltpu.make_async_copy(refs[k], refs[half + k], sems.at[k]) for k in range(half)]
    for copy in copies:
        copy.start()
    for copy in copies:
        copy.wait()


def publish(arrays):
    hbm = pl.BlockSpec(memory_space=pltpu.HBM)
    return pl.pallas_call(
        publish_kernel,
        out_shape=tuple(jax.ShapeDtypeStruct(x.shape, x.dtype) for x in arrays),
        in_specs=[pl.BlockSpec(memory_space=pltpu.VMEM)] * len(arrays),
        out_specs=(hbm,) * len(arrays),
        scratch_shapes=[pltpu.SemaphoreType.DMA((len(arrays),))],
        name="publish",
    )(*[pltpu.with_memory_space_constraint(x, pltpu.VMEM) for x in arrays])


def shards(rows, ys, zs, doc_scores, doc_labels, doc_ranks, query_tiles, bin_codes):
    tile_of = lambda x: x.reshape(8, LANES)
    gradient, hessian, histogram, split_gain = one_round(
        rows, ys, zs, query_tiles, tile_of(doc_scores), tile_of(doc_labels), tile_of(doc_ranks), bin_codes)
    gradient, hessian, histogram, split_gain = publish((gradient, hessian, histogram, split_gain))
    return gradient.reshape(-1), hessian.reshape(-1), histogram, split_gain.reshape(-1)


def solution(mesh):
    return jax.shard_map(
        functools.partial(shards, mesh.shape["row"], 4, mesh.shape["feat"] // 4),
        mesh=mesh,
        in_specs=(P(("row", "feat")), P(("row", "feat")), P(("row", "feat")), P("row", None), P("feat", "row")),
        out_specs=(P(("row", "feat")), P(("row", "feat")), P("feat", None, None), P("feat")),
        check_vma=False,
    )
```

```python
import functools

import jax
import jax.experimental.pallas as pl
import jax.experimental.pallas.tpu as pltpu
import jax.numpy as jnp
from jax import lax
from jax.sharding import PartitionSpec as P

BINS = 256
MAX_TILES = 8
LANES = 128
QUERIES = 64
HIGH, LOW = 8, 32
GROUP = 8
MESH = pl.DeviceIdType.MESH
F32, BF16, F8, I8 = jnp.float32, jnp.bfloat16, jnp.float8_e4m3fn, jnp.int8


def iota(shape, dim):
    return lax.broadcasted_iota(jnp.int32, shape, dim)


def pieces(x):
    first = x.astype(BF16)
    rest = x - first.astype(F32)
    second = rest.astype(BF16)
    third = (rest - second.astype(F32)).astype(BF16)
    return first, second, third


def query_spans(tiles_ref, me):
    first = [jnp.int32(0)] * 8
    count = [jnp.int32(1)] * 8
    start = 8 - me * 8
    for query in range(QUERIES):
        tiles = tiles_ref[0, query]
        for tile in range(8):
            inside = start <= 8 + tile
            first[tile] = jnp.where(inside, start, first[tile])
            count[tile] = jnp.where(inside, tiles, count[tile])
        start = start + tiles
    return first, count


def discount_table():
    place = (iota((8, LANES), 0) * LANES + iota((8, LANES), 1)).astype(F32)
    return place, 1.0 / jnp.log2(place + 2.0)


def span_rows(first, count):
    rows = iota((8, LANES), 0)
    first_rows, count_rows = jnp.zeros((8, LANES), jnp.int32), jnp.zeros((8, LANES), jnp.int32)
    for tile in range(8):
        first_rows = jnp.where(rows == tile, first[tile], first_rows)
        count_rows = jnp.where(rows == tile, count[tile], count_rows)
    return first_rows, count_rows


def query_scale(window, first_rows, count_rows, place, table):
    all_gains = window[1]
    reach = jnp.concatenate([(all_gains >= F32(2 ** level - 1)).astype(F32) for level in range(1, 5)], axis=0)
    reach = jnp.broadcast_to(jnp.sum(reach, axis=1, keepdims=True), (96, LANES))
    above = [jnp.zeros((8, LANES), F32)] * 4
    for tile in range(24):
        member = (first_rows <= tile) & (first_rows + count_rows > tile)
        for level in range(4):
            at = level * 24 + tile
            above[level] = above[level] + jnp.where(member, jnp.broadcast_to(reach[at:at + 1], (8, LANES)), 0.0)
    ideals = []
    for tile in range(8):
        total = jnp.zeros((8, LANES), F32)
        for level in range(4):
            limit = jnp.broadcast_to(above[level][tile:tile + 1], (8, LANES))
            total = total + jnp.where(place < limit, table * F32(2 ** level), 0.0)
        ideals.append(jnp.sum(total, axis=0, keepdims=True))
    ideal = jnp.sum(jnp.concatenate(ideals, axis=0), axis=1, keepdims=True)
    return 1.0 / (1.0 + ideal)


def widen(window, wide, slot):
    for which in range(3):
        turned = jnp.transpose(window[which, slot * 8:slot * 8 + 8, :])
        for tile in range(8):
            wide[which, slot * 8 + tile] = jnp.broadcast_to(turned[:, tile:tile + 1], (LANES, LANES))


def pair_sums(own, wide, first, count):
    odds, gains, discs = own
    grads, hessians = [], []
    rows = 32
    for tile in range(8):
        odds_i, gain_i, disc_i = (jnp.broadcast_to(x[tile:tile + 1], (rows, LANES)) for x in own)

        def column(step, carried):
            at = jnp.where(step < count[tile], jnp.minimum(jnp.maximum(first[tile] + step, 0), 23), 24)
            grad, hess = carried
            for part in range(0, LANES, rows):
                odds_j, gain_j, disc_j = (wide[which, at, part:part + rows, :] for which in range(3))
                inverse = pl.reciprocal(odds_i + odds_j, approx=True)
                delta = gain_i - gain_j
                weight = delta * (jnp.abs(disc_i - disc_j) * inverse)
                grad = grad + weight * jnp.where(delta > 0, odds_j, odds_i)
                hess = hess + jnp.abs(weight) * (inverse * odds_j)
            return grad, hess

        empty = jnp.zeros((rows, LANES), F32)
        grad, hess = lax.fori_loop(0, MAX_TILES, column, (empty, empty), unroll=8)
        grads.append(jnp.sum(grad, axis=0, keepdims=True))
        hessians.append(jnp.sum(hess, axis=0, keepdims=True))
    return jnp.concatenate(grads, axis=0), jnp.concatenate(hessians, axis=0)


def build_matrices(matrices):
    source, target = iota((BINS, BINS), 0), iota((BINS, BINS), 1)
    source_low, source_feat = source >> 3, source & 7
    target_feat, target_low = target >> 5, target & 31
    same = source_feat == target_feat
    for k, flag in enumerate((same & (source_low == target_low), same & (source_low <= target_low), same)):
        matrices[k] = jnp.where(flag, F32(1), F32(0)).astype(BF16)
    pick = ((source & (LOW - 1)) == 0) & ((source >> 5) == (target & 7))
    matrices[3] = jnp.where(pick, F32(1), F32(0)).astype(BF16)


def round_kernel(rows, ys, zs, *refs):
    accumulators = ([pltpu.ACC(k % 2)((2 * HIGH * GROUP, BINS), F32) for k in range(rows)]
                    + [pltpu.ACC(mxu)((48, BINS), F32) for mxu in (0, 0, 1)] + [pltpu.ACC(1)((32, BINS), F32)])
    pl.run_scoped(lambda *accs: round_body(rows, ys, zs, accs[:rows], accs[rows:], *refs), *accumulators)


def round_body(rows, ys, zs, accs, small, tiles_hbm, score_hbm, label_hbm, rank_hbm, codes_hbm,
                 grad_ref, hess_ref, hist_ref, gain_ref,
                 tiles_ref, score_ref, label_ref, rank_ref, codes,
                 window, wide, gathered, spread, matrices, mine, parts, blocks, bests, tops,
                 in_sem, code_sem, halo_send, halo_recv, send_z, recv_z, send_y, recv_y,
                 send_a, recv_a, send_b, recv_b, send_c, recv_c, send_e, recv_e):
    row, feat = lax.axis_index("row"), lax.axis_index("feat")
    feats = ys * zs
    y, z = feat // zs, lax.rem(feat, zs)
    groups = codes.shape[0] // GROUP
    chunks = codes.shape[1] // 1024

    loads = [pltpu.make_async_copy(src, dst, in_sem.at[k]) for k, (src, dst) in enumerate(
        ((score_hbm, score_ref), (label_hbm, label_ref), (rank_hbm, rank_ref), (tiles_hbm, tiles_ref)))]
    for load in loads:
        load.start()
    y_low, y_high = lax.rem(y, 2), y // 2

    def y_block(step):
        return lax.rem(y_high + step // 2, 2) * 2 + lax.rem(y_low + step % 2, 2)

    def code_load(step):
        docs = pl.ds(pl.multiple_of(y_block(step) * (zs * 1024), zs * 1024), zs * 1024)
        return pltpu.make_async_copy(codes_hbm.at[:, docs], codes.at[:, docs], code_sem.at[step])


    barrier = pltpu.get_barrier_semaphore()

    def at_row(step):
        return {"row": lax.rem(row + step, rows)}

    def at_z(step):
        return {"feat": y * zs + lax.rem(z + step, zs)}

    def at_y(step):
        return {"feat": y_block(step) * zs + z}

    def at_row_y(step):
        return {"row": lax.rem(row + step // 2, rows), "feat": y_block(step % 2) * zs + z}

    def at_z_y(step):
        return {"feat": y_block(step % 2 * 2) * zs + lax.rem(z + step // 2, zs)}

    def at_feat(step):
        return {"feat": lax.rem(feat + step, feats)}

    def signal(device):
        pl.semaphore_signal(barrier, inc=1, device_id=device, device_id_type=MESH)

    signal(at_feat(1))
    signal(at_feat(feats - 1))
    for step in range(1, 2 * zs):
        signal(at_z_y(step))
    signal(at_y(3))
    for step in range(1, 2 * rows):
        signal(at_row_y(step))
    for load in loads:
        load.wait()

    odds = jnp.exp(score_ref[...])
    gains = (jnp.left_shift(1, label_ref[...]) - 1).astype(F32)
    discs = 1.0 / jnp.log2(rank_ref[...].astype(F32) + 2.0)
    own = (odds, gains, discs)
    for which in range(3):
        window[which, 8:16, :] = own[which]
    pl.semaphore_wait(barrier, 2 + 2 * zs - 1 + 1 + 2 * rows - 1)
    halos = []
    for side, (target, place) in enumerate(((feats - 1, 16), (1, 0))):
        copy = pltpu.make_async_remote_copy(
            src_ref=window.at[:, pl.ds(8, 8), :], dst_ref=window.at[:, pl.ds(place, 8), :],
            send_sem=halo_send.at[side], recv_sem=halo_recv.at[side],
            device_id=at_feat(target), device_id_type=MESH)
        copy.start()
        halos.append(copy)
    code_load(0).start()
    for which, value in enumerate((0.0, -1.0, 0.0)):
        wide[which, 24] = jnp.full((LANES, LANES), value, F32)
    build_matrices(matrices)
    first, count = query_spans(tiles_ref, feat)
    span = span_rows(first, count)
    place, table = discount_table()
    widen(window, wide, 1)
    for copy in halos:
        copy.wait()
    code_load(1).start()
    widen(window, wide, 0)
    widen(window, wide, 2)
    scale = query_scale(window, *span, place, table)
    grad, hess = pair_sums(own, wide, first, count)
    grad = -grad * scale
    hess = hess * (odds * scale)
    grad_ref[...] = grad
    hess_ref[...] = hess
    gathered[feat] = jnp.concatenate([grad, hess], axis=0).astype(BF16)

    def over_z(step):
        return pltpu.make_async_remote_copy(
            src_ref=gathered.at[feat], dst_ref=gathered.at[feat], send_sem=send_z.at[step], recv_sem=recv_z.at[step],
            device_id=at_z(step), device_id_type=MESH)

    def over_y(step):
        block = gathered.at[pl.ds(y * zs, zs)]
        return pltpu.make_async_remote_copy(
            src_ref=block, dst_ref=block, send_sem=send_y.at[step], recv_sem=recv_y.at[step],
            device_id=at_y(step), device_id_type=MESH)

    offsets = [(turn + 1) // 2 if turn % 2 else zs - turn // 2 for turn in range(1, zs)]
    for step in offsets:
        over_z(step).start()
    code_load(0).wait()

    def scatter(group):
        return pltpu.make_async_remote_copy(
            src_ref=mine.at[group], dst_ref=parts.at[row], send_sem=send_a.at[group], recv_sem=recv_a.at[row],
            device_id={"row": jnp.int32(group)}, device_id_type=MESH)

    def arrival(step):
        source = lax.rem(row + step, rows)
        return pltpu.make_async_remote_copy(
            src_ref=parts.at[source], dst_ref=parts.at[source], send_sem=send_a.at[source], recv_sem=recv_a.at[source],
            device_id=at_row(step), device_id_type=MESH)

    zero = jnp.zeros((), BF16)

    def arrived(offset):
        over_z(zs - offset).wait_recv()

    def owner_of(turn):
        inner = lax.rem(turn, zs)
        odd = lax.rem(inner, 2)
        offset = odd * ((inner + 1) // 2) + (1 - odd) * (zs - inner // 2)
        outer = turn // zs
        owner_y = lax.rem(y_high + outer // 2, 2) * 2 + lax.rem(y_low + lax.rem(outer, 2), 2)
        return owner_y * zs + lax.rem(z + offset, zs)

    def add_chunks(owners):
        for slot, owner in enumerate(owners):
            part = gathered[owner].astype(F32)
            for which in range(2):
                for tile in range(8):
                    line = which * 8 + tile
                    at = slot * 1024 + tile * LANES
                    spread[which, :, at:at + LANES] = jnp.broadcast_to(part[line:line + 1], (16, LANES)).astype(BF16)
        for slot, owner in enumerate(owners):
            for k in range(1024 // BINS):
                at = pl.ds(pl.multiple_of(owner * 1024 + k * BINS, BINS), BINS)
                there = slot * 1024 + k * BINS
                lam = [spread[which, :, there:there + BINS] for which in range(2)]
                for group in range(groups):
                    code = codes[group * GROUP:(group + 1) * GROUP, at]
                    high = (code >> 5).astype(F32)
                    high = jnp.concatenate([high, high - 1.0], axis=0).astype(BF16)
                    hits = [high == jnp.array(2 * k, BF16) for k in range(HIGH // 2)]
                    lhs = jnp.concatenate([jnp.where(hit, value, zero) for value in lam for hit in hits], axis=0)
                    low = code & (LOW - 1)
                    low = jnp.concatenate([low - k for k in range(4)], axis=0).astype(I8)
                    rhs = jnp.concatenate(
                        [jnp.where(low == jnp.array(4 * k, I8), jnp.ones((), F8), jnp.zeros((), F8))
                         for k in range(LOW // 4)], axis=0)
                    pltpu.matmul_push_rhs(rhs, 0, group % 2, transpose=True)
                    pltpu.matmul_acc_lhs(accs[group], lhs, load_staged_rhs=0)

    @pl.loop(0, 2)
    def _(turn):
        @pl.when(turn == 1)
        def _():
            arrived(offsets[0])

        add_chunks([owner_of(turn)])

    for offset in offsets[1:3]:
        arrived(offset)
    add_chunks([owner_of(jnp.int32(turn)) for turn in (2, 3)])
    for offset in offsets[3:]:
        arrived(offset)
    for step in range(1, ys):
        over_y(step).start()
    for step in range(2, ys):
        code_load(step).start()

    @pl.loop(1, chunks // 4)
    def _(four):
        turn = 4 * four
        for step in range(1, ys):
            @pl.when(turn == step * zs)
            def _():
                over_y(step).wait_recv()
                code_load(step).wait()

        add_chunks([owner_of(turn + k) for k in range(4)])

    shape = (2 * HIGH, GROUP, BINS)
    same = iota(shape, 1) == (iota(shape, 2) & (GROUP - 1))
    for batch in range(0, groups, 4):
        for group in range(batch, batch + 4):
            total = pltpu.matmul_pop(accs[group]).reshape(shape)
            mine[group] = jnp.sum(jnp.where(same, total, 0.0), axis=1)
        for group in range(batch, batch + 4):
            @pl.when(row != group)
            def _():
                scatter(group).start()

    for k, mxu, stage in ((1, 0, 0), (2, 1, 0), (0, 0, 1), (3, 1, 1)):
        pltpu.matmul_push_rhs(matrices[k], stage, mxu)
    for step in range(1, zs):
        over_z(step).wait_send()
    for step in range(1, ys):
        over_y(step).wait_send()
    parts[row] = mine[row]
    for step in range(1, rows):
        arrival(step).wait_recv()
    summed = parts[0]
    for k in range(1, rows):
        summed = summed + parts[k]

    split = jnp.concatenate(pieces(summed), axis=0)
    for k, stage in ((1, 0), (2, 0), (0, 1)):
        pltpu.matmul_acc_lhs(small[k], split, load_staged_rhs=stage)

    def product(k):
        full = pltpu.matmul_pop(small[k])
        return full[0:16] + (full[16:32] + full[32:48])

    left, across, moved = product(1), product(2), product(0)
    running = [jnp.zeros((1, BINS), F32)] * 2
    sides = [[], []]
    for which in range(2):
        for k in range(HIGH):
            at = which * HIGH + k
            sides[which].append(left[at:at + 1] + running[which])
            running[which] = running[which] + across[at:at + 1]
    grad_left, hess_left = (jnp.concatenate(side, axis=0) for side in sides)
    grad_all, hess_all = running
    grad_right = grad_all - grad_left
    gain = (grad_left * grad_left / (hess_left + 1.0)
            + grad_right * grad_right / (hess_all - hess_left + 1.0)
            - grad_all * grad_all / (hess_all + 1.0))
    shape = (HIGH, BINS)
    last = (iota(shape, 0) == HIGH - 1) & ((iota(shape, 1) & (LOW - 1)) == LOW - 1)
    gain = jnp.where(last, -jnp.inf, gain)
    place_a = row * 2 + y_low
    bests[place_a] = jnp.max(gain, axis=0, keepdims=True)

    def send_best(step):
        return pltpu.make_async_remote_copy(
            src_ref=bests.at[place_a], dst_ref=bests.at[place_a], send_sem=send_b.at[step], recv_sem=recv_b.at[step],
            device_id=at_row_y(step), device_id_type=MESH)

    for step in range(1, 2 * rows):
        send_best(step).start()

    def send_block(step):
        return pltpu.make_async_remote_copy(
            src_ref=blocks.at[row], dst_ref=blocks.at[row], send_sem=send_e.at[step], recv_sem=recv_e.at[step],
            device_id=at_row(step), device_id_type=MESH)

    block = (iota(shape, 1) >> 5) == iota(shape, 0)
    for which in range(2):
        whole_rows = moved[which * HIGH:(which + 1) * HIGH]
        placed = jnp.zeros(shape, F32)
        for shift in range(GROUP):
            turned = whole_rows if shift == 0 else pltpu.roll(whole_rows, shift * LOW, 1)
            turned = jnp.where(block, turned, 0.0)
            placed = placed + (turned if shift == 0 else pltpu.roll(turned, GROUP - shift, 0))
        blocks[row, :, which, :] = placed

    for step in range(1, 2 * rows):
        send_best(step).wait()
    top = jnp.max(bests[...], axis=0)
    place_b = z * 2 + y_high
    tops[place_b] = jnp.broadcast_to(jnp.max(top, axis=1, keepdims=True), (1, LANES))

    def send_top(step):
        return pltpu.make_async_remote_copy(
            src_ref=tops.at[place_b], dst_ref=tops.at[place_b], send_sem=send_c.at[step], recv_sem=recv_c.at[step],
            device_id=at_z_y(step), device_id_type=MESH)

    for step in range(1, 2 * zs):
        send_top(step).start()
    for step in range(1, rows):
        send_block(step).start()
    every = jnp.concatenate([bests[k * 2 + y_low] for k in range(rows)], axis=0)
    for shift in (1, 2, 4, 8, 16):
        every = jnp.maximum(every, pltpu.roll(every, BINS - shift, 1))
    every = jnp.where((iota((rows, BINS), 1) & (LOW - 1)) == 0, every, 0.0)
    split = jnp.concatenate([piece.astype(F32) for piece in pieces(every)] + [jnp.zeros((rows, BINS), F32)], axis=0)
    pltpu.matmul_acc_lhs(small[3], split.astype(BF16), load_staged_rhs=1)
    full = pltpu.matmul_pop(small[3])
    chosen = full[0:rows] + (full[rows:2 * rows] + full[2 * rows:3 * rows])
    owned = (iota((rows, BINS), 1) >> 3) == iota((rows, BINS), 0)
    line = jnp.sum(jnp.where(owned, chosen, 0.0), axis=0, keepdims=True)
    for step in range(1, rows):
        send_block(step).wait()
    for k in range(rows):
        hist_ref[k * GROUP:(k + 1) * GROUP] = blocks[k]
    for group in range(groups):
        @pl.when(row != group)
        def _():
            scatter(group).wait_send()
    for step in range(1, 2 * zs):
        send_top(step).wait()
    largest = jnp.max(tops[...], axis=0)
    gain_ref[...] = (line[:, :LANES] / (largest + 1e-6))[:, :rows * GROUP]


def one_round(rows, ys, zs, tiles, scores, labels, ranks, codes):
    vmem = pl.BlockSpec(memory_space=pltpu.VMEM)
    hbm = pl.BlockSpec(memory_space=pltpu.HBM)
    here, docs = codes.shape
    groups = here // GROUP
    feats = ys * zs
    block = pltpu.VMEM((8, LANES), F32)
    dma = pltpu.SemaphoreType.DMA
    pair = lambda n: [dma((n,)), dma((n,))]
    return pl.pallas_call(
        functools.partial(round_kernel, rows, ys, zs),
        out_shape=(block, block, pltpu.VMEM((here, 2, BINS), F32), pltpu.VMEM((1, here), F32)),
        in_specs=[hbm] * 5,
        out_specs=(vmem,) * 4,
        scratch_shapes=[
            pltpu.SMEM((1, QUERIES), jnp.int32), pltpu.VMEM((8, LANES), F32), pltpu.VMEM((8, LANES), jnp.int32),
            pltpu.VMEM((8, LANES), jnp.int32), pltpu.VMEM((here, docs), jnp.int32),
            pltpu.VMEM((3, 24, LANES), F32), pltpu.VMEM((3, 25, LANES, LANES), F32), pltpu.VMEM((feats, 16, LANES), BF16),
            pltpu.VMEM((2, 16, 4096), BF16), pltpu.VMEM((4, BINS, BINS), BF16),
            pltpu.VMEM((groups, 2 * HIGH, BINS), F32), pltpu.VMEM((rows, 2 * HIGH, BINS), F32),
            pltpu.VMEM((rows, GROUP, 2, BINS), F32), pltpu.VMEM((2 * rows, 1, BINS), F32),
            pltpu.VMEM((2 * zs, 1, LANES), F32),
            dma((4,)), dma((ys,)), *pair(2), *pair(zs), *pair(ys),
            *pair(rows), *pair(2 * rows), *pair(2 * zs), *pair(rows),
        ],
        compiler_params=pltpu.CompilerParams(collective_id=0, has_side_effects=True, vmem_limit_bytes=60 * 2 ** 20),
        name="round",
    )(tiles, scores, labels, ranks, codes)


def publish_kernel(*refs):
    sems = refs[-1]
    half = (len(refs) - 1) // 2
    copies = [pltpu.make_async_copy(refs[k], refs[half + k], sems.at[k]) for k in range(half)]
    for copy in copies:
        copy.start()
    for copy in copies:
        copy.wait()


def publish(arrays):
    hbm = pl.BlockSpec(memory_space=pltpu.HBM)
    return pl.pallas_call(
        publish_kernel,
        out_shape=tuple(jax.ShapeDtypeStruct(x.shape, x.dtype) for x in arrays),
        in_specs=[pl.BlockSpec(memory_space=pltpu.VMEM)] * len(arrays),
        out_specs=(hbm,) * len(arrays),
        scratch_shapes=[pltpu.SemaphoreType.DMA((len(arrays),))],
        name="publish",
    )(*[pltpu.with_memory_space_constraint(x, pltpu.VMEM) for x in arrays])


def shards(rows, ys, zs, doc_scores, doc_labels, doc_ranks, query_tiles, bin_codes):
    tile_of = lambda x: x.reshape(8, LANES)
    gradient, hessian, histogram, split_gain = one_round(
        rows, ys, zs, query_tiles, tile_of(doc_scores), tile_of(doc_labels), tile_of(doc_ranks), bin_codes)
    gradient, hessian, histogram, split_gain = publish((gradient, hessian, histogram, split_gain))
    return gradient.reshape(-1), hessian.reshape(-1), histogram, split_gain.reshape(-1)


def solution(mesh):
    return jax.shard_map(
        functools.partial(shards, mesh.shape["row"], 4, mesh.shape["feat"] // 4),
        mesh=mesh,
        in_specs=(P(("row", "feat")), P(("row", "feat")), P(("row", "feat")), P("row", None), P("feat", "row")),
        out_specs=(P(("row", "feat")), P(("row", "feat")), P("feat", None, None), P("feat")),
        check_vma=False,
    )
```

```python
import functools

import jax
import jax.experimental.pallas as pl
import jax.experimental.pallas.tpu as pltpu
import jax.numpy as jnp
from jax import lax
from jax.sharding import PartitionSpec as P

BINS = 256
MAX_TILES = 8
LANES = 128
QUERIES = 64
HIGH, LOW = 8, 32
GROUP = 8
MESH = pl.DeviceIdType.MESH
F32, BF16, F8, I8 = jnp.float32, jnp.bfloat16, jnp.float8_e4m3fn, jnp.int8


def iota(shape, dim):
    return lax.broadcasted_iota(jnp.int32, shape, dim)


def pieces(x):
    first = x.astype(BF16)
    rest = x - first.astype(F32)
    second = rest.astype(BF16)
    third = (rest - second.astype(F32)).astype(BF16)
    return first, second, third


def query_spans(tiles_ref, me):
    first = [jnp.int32(0)] * 8
    count = [jnp.int32(1)] * 8
    start = 8 - me * 8
    for query in range(QUERIES):
        tiles = tiles_ref[0, query]
        for tile in range(8):
            inside = start <= 8 + tile
            first[tile] = jnp.where(inside, start, first[tile])
            count[tile] = jnp.where(inside, tiles, count[tile])
        start = start + tiles
    return first, count


def discount_table():
    place = (iota((8, LANES), 0) * LANES + iota((8, LANES), 1)).astype(F32)
    return place, 1.0 / jnp.log2(place + 2.0)


def span_rows(first, count):
    rows = iota((8, LANES), 0)
    first_rows, count_rows = jnp.zeros((8, LANES), jnp.int32), jnp.zeros((8, LANES), jnp.int32)
    for tile in range(8):
        first_rows = jnp.where(rows == tile, first[tile], first_rows)
        count_rows = jnp.where(rows == tile, count[tile], count_rows)
    return first_rows, count_rows


def query_scale(window, first_rows, count_rows, place, table):
    all_gains = window[1]
    reach = jnp.concatenate([(all_gains >= F32(2 ** level - 1)).astype(F32) for level in range(1, 5)], axis=0)
    reach = jnp.broadcast_to(jnp.sum(reach, axis=1, keepdims=True), (96, LANES))
    above = [jnp.zeros((8, LANES), F32)] * 4
    for tile in range(24):
        member = (first_rows <= tile) & (first_rows + count_rows > tile)
        for level in range(4):
            at = level * 24 + tile
            above[level] = above[level] + jnp.where(member, jnp.broadcast_to(reach[at:at + 1], (8, LANES)), 0.0)
    ideals = []
    for tile in range(8):
        total = jnp.zeros((8, LANES), F32)
        for level in range(4):
            limit = jnp.broadcast_to(above[level][tile:tile + 1], (8, LANES))
            total = total + jnp.where(place < limit, table * F32(2 ** level), 0.0)
        ideals.append(jnp.sum(total, axis=0, keepdims=True))
    ideal = jnp.sum(jnp.concatenate(ideals, axis=0), axis=1, keepdims=True)
    return 1.0 / (1.0 + ideal)


def widen(window, wide, slot):
    for which in range(3):
        turned = jnp.transpose(window[which, slot * 8:slot * 8 + 8, :])
        for tile in range(8):
            wide[which, slot * 8 + tile] = jnp.broadcast_to(turned[:, tile:tile + 1], (LANES, LANES))


def pair_sums(own, wide, first, count):
    odds, gains, discs = own
    grads, hessians = [], []
    rows = 32
    for tile in range(8):
        odds_i, gain_i, disc_i = (jnp.broadcast_to(x[tile:tile + 1], (rows, LANES)) for x in own)

        def column(step, carried):
            at = jnp.where(step < count[tile], jnp.minimum(jnp.maximum(first[tile] + step, 0), 23), 24)
            grad, hess = carried
            for part in range(0, LANES, rows):
                odds_j, gain_j, disc_j = (wide[which, at, part:part + rows, :] for which in range(3))
                inverse = pl.reciprocal(odds_i + odds_j, approx=True)
                delta = gain_i - gain_j
                weight = delta * (jnp.abs(disc_i - disc_j) * inverse)
                grad = grad + weight * jnp.where(delta > 0, odds_j, odds_i)
                hess = hess + jnp.abs(weight) * (inverse * odds_j)
            return grad, hess

        empty = jnp.zeros((rows, LANES), F32)
        grad, hess = lax.fori_loop(0, MAX_TILES, column, (empty, empty), unroll=8)
        grads.append(jnp.sum(grad, axis=0, keepdims=True))
        hessians.append(jnp.sum(hess, axis=0, keepdims=True))
    return jnp.concatenate(grads, axis=0), jnp.concatenate(hessians, axis=0)


def build_matrices(matrices):
    source, target = iota((BINS, BINS), 0), iota((BINS, BINS), 1)
    source_low, source_feat = source >> 3, source & 7
    target_feat, target_low = target >> 5, target & 31
    same = source_feat == target_feat
    for k, flag in enumerate((same & (source_low == target_low), same & (source_low <= target_low), same)):
        matrices[k] = jnp.where(flag, F32(1), F32(0)).astype(BF16)
    pick = ((source & (LOW - 1)) == 0) & ((source >> 5) == (target & 7))
    matrices[3] = jnp.where(pick, F32(1), F32(0)).astype(BF16)


def round_kernel(rows, ys, zs, *refs):
    accumulators = ([pltpu.ACC(k % 2)((2 * HIGH * GROUP, BINS), F32) for k in range(rows)]
                    + [pltpu.ACC(mxu)((48, BINS), F32) for mxu in (0, 0, 1)] + [pltpu.ACC(1)((32, BINS), F32)])
    pl.run_scoped(lambda *accs: round_body(rows, ys, zs, accs[:rows], accs[rows:], *refs), *accumulators)


def round_body(rows, ys, zs, accs, small, tiles_hbm, score_hbm, label_hbm, rank_hbm, codes_hbm,
                 grad_ref, hess_ref, hist_ref, gain_ref,
                 tiles_ref, score_ref, label_ref, rank_ref, codes,
                 window, wide, gathered, spread, matrices, mine, parts, blocks, bests, tops,
                 in_sem, code_sem, halo_send, halo_recv, send_z, recv_z, send_y, recv_y,
                 send_a, recv_a, send_b, recv_b, send_c, recv_c, send_e, recv_e):
    row, feat = lax.axis_index("row"), lax.axis_index("feat")
    feats = ys * zs
    y, z = feat // zs, lax.rem(feat, zs)
    groups = codes.shape[0] // GROUP
    chunks = codes.shape[1] // 1024

    loads = [pltpu.make_async_copy(src, dst, in_sem.at[k]) for k, (src, dst) in enumerate(
        ((score_hbm, score_ref), (label_hbm, label_ref), (rank_hbm, rank_ref), (tiles_hbm, tiles_ref)))]
    for load in loads:
        load.start()
    y_low, y_high = lax.rem(y, 2), y // 2

    def y_block(step):
        return lax.rem(y_high + step // 2, 2) * 2 + lax.rem(y_low + step % 2, 2)

    def code_load(step):
        docs = pl.ds(pl.multiple_of(y_block(step) * (zs * 1024), zs * 1024), zs * 1024)
        return pltpu.make_async_copy(codes_hbm.at[:, docs], codes.at[:, docs], code_sem.at[step])


    barrier = pltpu.get_barrier_semaphore()

    def at_row(step):
        return {"row": lax.rem(row + step, rows)}

    def at_z(step):
        return {"feat": y * zs + lax.rem(z + step, zs)}

    def at_y(step):
        return {"feat": y_block(step) * zs + z}

    def at_row_y(step):
        return {"row": lax.rem(row + step // 2, rows), "feat": y_block(step % 2) * zs + z}

    def at_z_y(step):
        return {"feat": y_block(step % 2 * 2) * zs + lax.rem(z + step // 2, zs)}

    def at_feat(step):
        return {"feat": lax.rem(feat + step, feats)}

    def signal(device):
        pl.semaphore_signal(barrier, inc=1, device_id=device, device_id_type=MESH)

    signal(at_feat(1))
    signal(at_feat(feats - 1))
    for step in range(1, 2 * zs):
        signal(at_z_y(step))
    signal(at_y(3))
    for step in range(1, 2 * rows):
        signal(at_row_y(step))
    for load in loads:
        load.wait()

    odds = jnp.exp(score_ref[...])
    gains = (jnp.left_shift(1, label_ref[...]) - 1).astype(F32)
    discs = 1.0 / jnp.log2(rank_ref[...].astype(F32) + 2.0)
    own = (odds, gains, discs)
    for which in range(3):
        window[which, 8:16, :] = own[which]
    pl.semaphore_wait(barrier, 2 + 2 * zs - 1 + 1 + 2 * rows - 1)
    halos = []
    for side, (target, place) in enumerate(((feats - 1, 16), (1, 0))):
        copy = pltpu.make_async_remote_copy(
            src_ref=window.at[:, pl.ds(8, 8), :], dst_ref=window.at[:, pl.ds(place, 8), :],
            send_sem=halo_send.at[side], recv_sem=halo_recv.at[side],
            device_id=at_feat(target), device_id_type=MESH)
        copy.start()
        halos.append(copy)
    code_load(0).start()
    for which, value in enumerate((0.0, -1.0, 0.0)):
        wide[which, 24] = jnp.full((LANES, LANES), value, F32)
    build_matrices(matrices)
    first, count = query_spans(tiles_ref, feat)
    span = span_rows(first, count)
    place, table = discount_table()
    widen(window, wide, 1)
    for copy in halos:
        copy.wait()
    for step in range(1, ys):
        code_load(step).start()
    widen(window, wide, 0)
    widen(window, wide, 2)
    scale = query_scale(window, *span, place, table)
    grad, hess = pair_sums(own, wide, first, count)
    grad = -grad * scale
    hess = hess * (odds * scale)
    grad_ref[...] = grad
    hess_ref[...] = hess
    gathered[feat] = jnp.concatenate([grad, hess], axis=0).astype(BF16)

    def over_z(step):
        return pltpu.make_async_remote_copy(
            src_ref=gathered.at[feat], dst_ref=gathered.at[feat], send_sem=send_z.at[step], recv_sem=recv_z.at[step],
            device_id=at_z(step), device_id_type=MESH)

    def over_y(step):
        block = gathered.at[pl.ds(y * zs, zs)]
        return pltpu.make_async_remote_copy(
            src_ref=block, dst_ref=block, send_sem=send_y.at[step], recv_sem=recv_y.at[step],
            device_id=at_y(step), device_id_type=MESH)

    offsets = [(turn + 1) // 2 if turn % 2 else zs - turn // 2 for turn in range(1, zs)]
    for step in offsets:
        over_z(step).start()
    code_load(0).wait()

    def scatter(group):
        return pltpu.make_async_remote_copy(
            src_ref=mine.at[group], dst_ref=parts.at[row], send_sem=send_a.at[group], recv_sem=recv_a.at[row],
            device_id={"row": jnp.int32(group)}, device_id_type=MESH)

    def arrival(step):
        source = lax.rem(row + step, rows)
        return pltpu.make_async_remote_copy(
            src_ref=parts.at[source], dst_ref=parts.at[source], send_sem=send_a.at[source], recv_sem=recv_a.at[source],
            device_id=at_row(step), device_id_type=MESH)

    zero = jnp.zeros((), BF16)

    def arrived(offset):
        over_z(zs - offset).wait_recv()

    def owner_of(turn):
        inner = lax.rem(turn, zs)
        odd = lax.rem(inner, 2)
        offset = odd * ((inner + 1) // 2) + (1 - odd) * (zs - inner // 2)
        outer = turn // zs
        owner_y = lax.rem(y_high + outer // 2, 2) * 2 + lax.rem(y_low + lax.rem(outer, 2), 2)
        return owner_y * zs + lax.rem(z + offset, zs)

    def add_chunks(owners):
        for slot, owner in enumerate(owners):
            part = gathered[owner].astype(F32)
            for which in range(2):
                for tile in range(8):
                    line = which * 8 + tile
                    at = slot * 1024 + tile * LANES
                    spread[which, :, at:at + LANES] = jnp.broadcast_to(part[line:line + 1], (16, LANES)).astype(BF16)
        for slot, owner in enumerate(owners):
            for k in range(1024 // BINS):
                at = pl.ds(pl.multiple_of(owner * 1024 + k * BINS, BINS), BINS)
                there = slot * 1024 + k * BINS
                lam = [spread[which, :, there:there + BINS] for which in range(2)]
                for group in range(groups):
                    code = codes[group * GROUP:(group + 1) * GROUP, at]
                    high = (code >> 5).astype(F32)
                    high = jnp.concatenate([high, high - 1.0], axis=0).astype(BF16)
                    hits = [high == jnp.array(2 * k, BF16) for k in range(HIGH // 2)]
                    lhs = jnp.concatenate([jnp.where(hit, value, zero) for value in lam for hit in hits], axis=0)
                    low = code & (LOW - 1)
                    low = jnp.concatenate([low - k for k in range(4)], axis=0).astype(I8)
                    rhs = jnp.concatenate(
                        [jnp.where(low == jnp.array(4 * k, I8), jnp.ones((), F8), jnp.zeros((), F8))
                         for k in range(LOW // 4)], axis=0)
                    pltpu.matmul_push_rhs(rhs, 0, group % 2, transpose=True)
                    pltpu.matmul_acc_lhs(accs[group], lhs, load_staged_rhs=0)

    @pl.loop(0, 2)
    def _(turn):
        @pl.when(turn == 1)
        def _():
            arrived(offsets[0])

        add_chunks([owner_of(turn)])

    for offset in offsets[1:3]:
        arrived(offset)
    add_chunks([owner_of(jnp.int32(turn)) for turn in (2, 3)])
    for offset in offsets[3:]:
        arrived(offset)
    for step in range(1, ys):
        over_y(step).start()

    @pl.loop(1, chunks // 4)
    def _(four):
        turn = 4 * four
        for step in range(1, ys):
            @pl.when(turn == step * zs)
            def _():
                over_y(step).wait_recv()
                code_load(step).wait()

        add_chunks([owner_of(turn + k) for k in range(4)])

    shape = (2 * HIGH, GROUP, BINS)
    same = iota(shape, 1) == (iota(shape, 2) & (GROUP - 1))
    for batch in range(0, groups, 4):
        for group in range(batch, batch + 4):
            total = pltpu.matmul_pop(accs[group]).reshape(shape)
            mine[group] = jnp.sum(jnp.where(same, total, 0.0), axis=1)
        for group in range(batch, batch + 4):
            @pl.when(row != group)
            def _():
                scatter(group).start()

    for k, mxu, stage in ((1, 0, 0), (2, 1, 0), (0, 0, 1), (3, 1, 1)):
        pltpu.matmul_push_rhs(matrices[k], stage, mxu)
    for step in range(1, zs):
        over_z(step).wait_send()
    for step in range(1, ys):
        over_y(step).wait_send()
    parts[row] = mine[row]
    for step in range(1, rows):
        arrival(step).wait_recv()
    summed = parts[0]
    for k in range(1, rows):
        summed = summed + parts[k]

    split = jnp.concatenate(pieces(summed), axis=0)
    for k, stage in ((1, 0), (2, 0), (0, 1)):
        pltpu.matmul_acc_lhs(small[k], split, load_staged_rhs=stage)

    def product(k):
        full = pltpu.matmul_pop(small[k])
        return full[0:16] + (full[16:32] + full[32:48])

    left, across, moved = product(1), product(2), product(0)
    running = [jnp.zeros((1, BINS), F32)] * 2
    sides = [[], []]
    for which in range(2):
        for k in range(HIGH):
            at = which * HIGH + k
            sides[which].append(left[at:at + 1] + running[which])
            running[which] = running[which] + across[at:at + 1]
    grad_left, hess_left = (jnp.concatenate(side, axis=0) for side in sides)
    grad_all, hess_all = running
    grad_right = grad_all - grad_left
    gain = (grad_left * grad_left / (hess_left + 1.0)
            + grad_right * grad_right / (hess_all - hess_left + 1.0)
            - grad_all * grad_all / (hess_all + 1.0))
    shape = (HIGH, BINS)
    last = (iota(shape, 0) == HIGH - 1) & ((iota(shape, 1) & (LOW - 1)) == LOW - 1)
    gain = jnp.where(last, -jnp.inf, gain)
    place_a = row * 2 + y_low
    bests[place_a] = jnp.max(gain, axis=0, keepdims=True)

    def send_best(step):
        return pltpu.make_async_remote_copy(
            src_ref=bests.at[place_a], dst_ref=bests.at[place_a], send_sem=send_b.at[step], recv_sem=recv_b.at[step],
            device_id=at_row_y(step), device_id_type=MESH)

    for step in range(1, 2 * rows):
        send_best(step).start()

    def send_block(step):
        return pltpu.make_async_remote_copy(
            src_ref=blocks.at[row], dst_ref=blocks.at[row], send_sem=send_e.at[step], recv_sem=recv_e.at[step],
            device_id=at_row(step), device_id_type=MESH)

    block = (iota(shape, 1) >> 5) == iota(shape, 0)
    for which in range(2):
        whole_rows = moved[which * HIGH:(which + 1) * HIGH]
        placed = jnp.zeros(shape, F32)
        for shift in range(GROUP):
            turned = whole_rows if shift == 0 else pltpu.roll(whole_rows, shift * LOW, 1)
            turned = jnp.where(block, turned, 0.0)
            placed = placed + (turned if shift == 0 else pltpu.roll(turned, GROUP - shift, 0))
        blocks[row, :, which, :] = placed

    for step in range(1, 2 * rows):
        send_best(step).wait()
    top = jnp.max(bests[...], axis=0)
    place_b = z * 2 + y_high
    tops[place_b] = jnp.broadcast_to(jnp.max(top, axis=1, keepdims=True), (1, LANES))

    def send_top(step):
        return pltpu.make_async_remote_copy(
            src_ref=tops.at[place_b], dst_ref=tops.at[place_b], send_sem=send_c.at[step], recv_sem=recv_c.at[step],
            device_id=at_z_y(step), device_id_type=MESH)

    for step in range(1, 2 * zs):
        send_top(step).start()
    for step in range(1, rows):
        send_block(step).start()
    every = jnp.concatenate([bests[k * 2 + y_low] for k in range(rows)], axis=0)
    for shift in (1, 2, 4, 8, 16):
        every = jnp.maximum(every, pltpu.roll(every, BINS - shift, 1))
    every = jnp.where((iota((rows, BINS), 1) & (LOW - 1)) == 0, every, 0.0)
    split = jnp.concatenate([piece.astype(F32) for piece in pieces(every)] + [jnp.zeros((rows, BINS), F32)], axis=0)
    pltpu.matmul_acc_lhs(small[3], split.astype(BF16), load_staged_rhs=1)
    full = pltpu.matmul_pop(small[3])
    chosen = full[0:rows] + (full[rows:2 * rows] + full[2 * rows:3 * rows])
    owned = (iota((rows, BINS), 1) >> 3) == iota((rows, BINS), 0)
    line = jnp.sum(jnp.where(owned, chosen, 0.0), axis=0, keepdims=True)
    for step in range(1, rows):
        send_block(step).wait()
    for k in range(rows):
        hist_ref[k * GROUP:(k + 1) * GROUP] = blocks[k]
    for group in range(groups):
        @pl.when(row != group)
        def _():
            scatter(group).wait_send()
    for step in range(1, 2 * zs):
        send_top(step).wait()
    largest = jnp.max(tops[...], axis=0)
    gain_ref[...] = (line[:, :LANES] / (largest + 1e-6))[:, :rows * GROUP]


def one_round(rows, ys, zs, tiles, scores, labels, ranks, codes):
    vmem = pl.BlockSpec(memory_space=pltpu.VMEM)
    hbm = pl.BlockSpec(memory_space=pltpu.HBM)
    here, docs = codes.shape
    groups = here // GROUP
    feats = ys * zs
    block = pltpu.VMEM((8, LANES), F32)
    dma = pltpu.SemaphoreType.DMA
    pair = lambda n: [dma((n,)), dma((n,))]
    return pl.pallas_call(
        functools.partial(round_kernel, rows, ys, zs),
        out_shape=(block, block, pltpu.VMEM((here, 2, BINS), F32), pltpu.VMEM((1, here), F32)),
        in_specs=[hbm] * 5,
        out_specs=(vmem,) * 4,
        scratch_shapes=[
            pltpu.SMEM((1, QUERIES), jnp.int32), pltpu.VMEM((8, LANES), F32), pltpu.VMEM((8, LANES), jnp.int32),
            pltpu.VMEM((8, LANES), jnp.int32), pltpu.VMEM((here, docs), jnp.int32),
            pltpu.VMEM((3, 24, LANES), F32), pltpu.VMEM((3, 25, LANES, LANES), F32), pltpu.VMEM((feats, 16, LANES), BF16),
            pltpu.VMEM((2, 16, 4096), BF16), pltpu.VMEM((4, BINS, BINS), BF16),
            pltpu.VMEM((groups, 2 * HIGH, BINS), F32), pltpu.VMEM((rows, 2 * HIGH, BINS), F32),
            pltpu.VMEM((rows, GROUP, 2, BINS), F32), pltpu.VMEM((2 * rows, 1, BINS), F32),
            pltpu.VMEM((2 * zs, 1, LANES), F32),
            dma((4,)), dma((ys,)), *pair(2), *pair(zs), *pair(ys),
            *pair(rows), *pair(2 * rows), *pair(2 * zs), *pair(rows),
        ],
        compiler_params=pltpu.CompilerParams(collective_id=0, has_side_effects=True, vmem_limit_bytes=60 * 2 ** 20),
        name="round",
    )(tiles, scores, labels, ranks, codes)


def publish_kernel(*refs):
    sems = refs[-1]
    half = (len(refs) - 1) // 2
    copies = [pltpu.make_async_copy(refs[k], refs[half + k], sems.at[k]) for k in range(half)]
    for copy in copies:
        copy.start()
    for copy in copies:
        copy.wait()


def publish(arrays):
    hbm = pl.BlockSpec(memory_space=pltpu.HBM)
    return pl.pallas_call(
        publish_kernel,
        out_shape=tuple(jax.ShapeDtypeStruct(x.shape, x.dtype) for x in arrays),
        in_specs=[pl.BlockSpec(memory_space=pltpu.VMEM)] * len(arrays),
        out_specs=(hbm,) * len(arrays),
        scratch_shapes=[pltpu.SemaphoreType.DMA((len(arrays),))],
        name="publish",
    )(*[pltpu.with_memory_space_constraint(x, pltpu.VMEM) for x in arrays])


def shards(rows, ys, zs, doc_scores, doc_labels, doc_ranks, query_tiles, bin_codes):
    tile_of = lambda x: x.reshape(8, LANES)
    gradient, hessian, histogram, split_gain = one_round(
        rows, ys, zs, query_tiles, tile_of(doc_scores), tile_of(doc_labels), tile_of(doc_ranks), bin_codes)
    gradient, hessian, histogram, split_gain = publish((gradient, hessian, histogram, split_gain))
    return gradient.reshape(-1), hessian.reshape(-1), histogram, split_gain.reshape(-1)


def solution(mesh):
    return jax.shard_map(
        functools.partial(shards, mesh.shape["row"], 4, mesh.shape["feat"] // 4),
        mesh=mesh,
        in_specs=(P(("row", "feat")), P(("row", "feat")), P(("row", "feat")), P("row", None), P("feat", "row")),
        out_specs=(P(("row", "feat")), P(("row", "feat")), P("feat", None, None), P("feat")),
        check_vma=False,
    )
```
